32 devices in a mesh: gx: 4 (over z), gy: 8 (over y, x, core).
Axes of the slice: x: 2, y: 2, z: 4, core: 2. Of those that a mesh axis runs over, the one named last changes fastest.
Arguments:
- pdf: float32 [19, 64, 1024], P(None, 'gx', 'gy'), as said below
- grains: float32 [26, 4, 2048], P(None, 'gx', 'gy'), as said below
- grain_moves: int32 [4, 2048], P('gx', 'gy'), may hold values from 0 to 8, as said below
- owner_map: int32 [8, 16], P('gx', 'gy'), may hold values from 0 to 3, as said below
- link_lists: int32 [3, 8, 4096], P(None, 'gx', 'gy'), may hold values from 0 to 511, as said below
Outputs:
- moved_blocks: float32 [16, 8, 19, 512], P('gx', 'gy')
- new_grains: float32 [26, 4, 2560], P(None, 'gx', 'gy')
The draws below stay inside these ranges and needn't reach their ends.
Inputs may be any that keep to these rules, and one draw needn't show every extreme that they name: `pdf`: each entry lies between 0.4 and 1.6 times its direction's lattice weight. `grains`: A grain's position lies inside the cells of the group that it belongs to after the move. `grain_moves`: at most 8 grains of one group move to any one of its eight neighbouring groups; every group moves at least one grain each way, and some group receives exactly 8 grains from each of its eight neighbours. `owner_map`: owners are gx indices in the block's own row of gy. At most 1 block of one group go to one owner, and in every row of gy one owner receives exactly 1 block from every group of that row. `link_lists`: row 0: a cell number of the block; row 1: a direction 1 to 18; row 2: a grain slot below 320. No cell appears twice among one block's links.
All inputs are finite; a program needn't handle non-finite values.
Results may differ from the reference program's by a relative error of at most 0.0003.
Values sent between devices are 32-bit elements; how exact they have to be, the bound alone decides.
A program may use at most 64 MiB of HBM per device.

```python
import jax
import jax.numpy as jnp
import numpy as np
from jax import lax

Q = 19
GV = 26
E = 8
Z = 8
BXD = 2
BYD = 2
GR = 256
GCAP = 8
CAPP = 1
LB = 256
GROUP = 4
LANES = 8
BLK = 4
SLOTS = 4
CB = 512
GSLOT = 320
NBX = 8
NBY = 16
NX = 64
NY = 128


lattice_wts = np.array([1.0 / 3.0] + [1.0 / 18.0] * 6 + [1.0 / 36.0] * 12, dtype=np.float32)


lattice_stepx = np.array([0, 1, -1, 0, 0, 0, 0, 1, -1, 1, -1, 1, -1, 1, -1, 0, 0, 0, 0], dtype=np.float32)


def draw_pdf(key, part):
    grid_shape = (Q, NX, NY * Z)
    weights = jnp.asarray(lattice_wts)[:, None, None]
    drift_term = jnp.asarray(lattice_stepx)[:, None, None]
    jitter = jax.random.uniform(key, grid_shape, jnp.float32, -1.0, 1.0)
    return weights * (1.0 + 0.15 * drift_term + 0.45 * jitter)


def draw_codes(key):
    base_key = jax.random.fold_in(key, 11)
    count_key, target_key, spread_key = jax.random.split(base_key, 3)
    counts = jax.random.randint(count_key, (GROUP, LANES, 9), GCAP // 2, GCAP + 1, jnp.int32)
    counts = counts.at[:, :, 4].set(0)
    aim_x = jax.random.randint(jax.random.fold_in(target_key, 1), (), 0, GROUP, jnp.int32)
    aim_y = jax.random.randint(jax.random.fold_in(target_key, 2), (), 0, LANES, jnp.int32)
    for move_code in (0, 1, 2, 3, 5, 6, 7, 8):
        counts = counts.at[(aim_x - (move_code // 3 - 1)) % GROUP, (aim_y - (move_code % 3 - 1)) % LANES, move_code].set(GCAP)
    group_keys = jax.random.split(spread_key, GROUP * LANES)
    flat_counts = counts.reshape(GROUP * LANES, 9)

    def one_group(group_key, group_counts):
        bounds = jnp.cumsum(group_counts, dtype=jnp.int32)
        ordinal = jnp.arange(GR, dtype=jnp.int32)
        sorted_codes = jnp.sum((ordinal[:, None] >= bounds[None, :]).astype(jnp.int32), axis=1, dtype=jnp.int32)
        sorted_codes = jnp.where(sorted_codes > 8, 4, sorted_codes)
        return jax.random.permutation(group_key, sorted_codes)
    grouped = jax.vmap(one_group)(group_keys, flat_counts)
    return grouped.reshape(GROUP, LANES, GR)


def draw_grain_moves(key, part):
    return draw_codes(key).reshape(GROUP, LANES * GR)


def draw_grains(key, part):
    grouped = draw_codes(key)
    dest_x = (jnp.arange(GROUP, dtype=jnp.int32)[:, None, None] + grouped // 3 - 1) % GROUP
    dest_y = (jnp.arange(LANES, dtype=jnp.int32)[None, :, None] + grouped % 3 - 1) % LANES
    float_key = jax.random.fold_in(key, 29)
    place_key, motion_key, remain_key = jax.random.split(float_key, 3)
    grid_shape = (GROUP, LANES, GR)
    fractions = jax.random.uniform(place_key, (3,) + grid_shape, jnp.float32)
    centre_x = (dest_x * (BXD * E)).astype(jnp.float32) + fractions[0] * (BXD * E)
    centre_y = (dest_y * (BYD * E)).astype(jnp.float32) + fractions[1] * (BYD * E)
    centre_z = fractions[2] * Z
    motion = jax.random.normal(motion_key, (6,) + grid_shape, jnp.float32)
    remaining = jax.random.normal(remain_key, (GV - 9,) + grid_shape, jnp.float32)
    scales = jnp.array([0.02, 0.02, 0.02, 0.0015, 0.0015, 0.0015], jnp.float32)[:, None, None, None]
    records = jnp.concatenate([jnp.stack([centre_x, centre_y, centre_z]), motion * scales, remaining], axis=0)
    return records.reshape(GV, GROUP, LANES * GR)


def draw_owner_map(key, part):
    heavy_owner = jax.random.randint(jax.random.fold_in(key, 5), (LANES,), 0, GROUP, jnp.int32)
    device_keys = jax.random.split(jax.random.fold_in(key, 6), GROUP * LANES)
    heavies = jnp.broadcast_to(heavy_owner[None, :], (GROUP, LANES)).reshape(-1)

    def one_device(device_key, chosen):
        first_key, second_key = jax.random.split(device_key)
        candidates = (chosen + 1 + jnp.arange(CAPP * (GROUP - 1), dtype=jnp.int32) // CAPP) % GROUP
        chosen_owners = jax.random.permutation(first_key, candidates)[:BLK - CAPP]
        heavy_part = jnp.full((CAPP,), chosen, jnp.int32)
        return jax.random.permutation(second_key, jnp.concatenate([heavy_part, chosen_owners]))
    owners = jax.vmap(one_device)(device_keys, heavies)
    return owners.reshape(GROUP, LANES, BXD, BYD).transpose(0, 2, 1, 3).reshape(GROUP * BXD, LANES * BYD)


def draw_link_lists(key, part):
    block_keys = jax.random.split(jax.random.fold_in(key, 7), NBX * NBY)

    def one_block(block_key):
        cell_key, dir_key, slot_key = jax.random.split(block_key, 3)
        cell_ids = jax.random.permutation(cell_key, CB)[:LB].astype(jnp.int32)
        direction_ids = jax.random.randint(dir_key, (LB,), 1, Q, jnp.int32)
        slot_ids = jax.random.randint(slot_key, (LB,), 0, GSLOT, jnp.int32)
        return jnp.stack([cell_ids, direction_ids, slot_ids])
    link_rows = jax.vmap(one_block)(block_keys)
    return link_rows.reshape(NBX, NBY, 3, LB).transpose(2, 0, 1, 3).reshape(3, NBX, NBY * LB)


def setup_inputs(seed: int = 0) -> dict:
    key_list = jax.random.split(jax.random.key(seed), 6)
    return {
        "pdf": draw_pdf(jax.random.fold_in(key_list[5], 71), 0),
        "grains": draw_grains(jax.random.fold_in(key_list[5], 71), 0),
        "grain_moves": draw_grain_moves(jax.random.fold_in(key_list[5], 71), 0),
        "owner_map": draw_owner_map(jax.random.fold_in(key_list[5], 71), 0),
        "link_lists": draw_link_lists(jax.random.fold_in(key_list[5], 71), 0),
    }


lattice_vel = np.array([[0, 0, 0], [1, 0, 0], [-1, 0, 0], [0, 1, 0], [0, -1, 0], [0, 0, 1], [0, 0, -1], [1, 1, 0], [-1, -1, 0], [1, -1, 0], [-1, 1, 0], [1, 0, 1], [-1, 0, -1], [1, 0, -1], [-1, 0, 1], [0, 1, 1], [0, -1, -1], [0, 1, -1], [0, -1, 1]], dtype=np.int32)
lattice_wts = np.array([1.0 / 3.0] + [1.0 / 18.0] * 6 + [1.0 / 36.0] * 12, dtype=np.float32)
opposite_dir = np.array([0, 2, 1, 4, 3, 6, 5, 8, 7, 10, 9, 12, 11, 14, 13, 16, 15, 18, 17], dtype=np.int32)
velocity_cols = lattice_vel.astype(np.float32)
moment_rows = np.stack([np.ones(19, np.float32), velocity_cols[:, 0], velocity_cols[:, 1], velocity_cols[:, 2], velocity_cols[:, 0] * velocity_cols[:, 0], velocity_cols[:, 1] * velocity_cols[:, 1], velocity_cols[:, 2] * velocity_cols[:, 2], velocity_cols[:, 0] * velocity_cols[:, 1], velocity_cols[:, 0] * velocity_cols[:, 2], velocity_cols[:, 1] * velocity_cols[:, 2]]).astype(np.float32)
viscosity_zero = 0.1
viscosity_limit = 0.01
relax_zero = 0.8
carreau_time = 20.0
carreau_power = 0.5

def collide(populations):
    moments = jnp.dot(jnp.asarray(moment_rows), populations, precision=lax.Precision.HIGHEST)
    density = moments[0]
    velocity = moments[1:4] / density
    projected = jnp.dot(jnp.asarray(velocity_cols), velocity, precision=lax.Precision.HIGHEST)
    speed_sq = lax.optimization_barrier(jnp.sum(velocity * velocity, axis=0))
    equilibrium = jnp.asarray(lattice_wts)[:, None] * density * (1.0 + 3.0 * projected + 4.5 * projected * projected - 1.5 * speed_sq)
    density_third = density / 3.0
    stress_xx = moments[4] - density_third - density * velocity[0] * velocity[0]
    stress_yy = moments[5] - density_third - density * velocity[1] * velocity[1]
    stress_zz = moments[6] - density_third - density * velocity[2] * velocity[2]
    stress_xy = moments[7] - density * velocity[0] * velocity[1]
    stress_xz = moments[8] - density * velocity[0] * velocity[2]
    stress_yz = moments[9] - density * velocity[1] * velocity[2]
    contracted = stress_xx * stress_xx + stress_yy * stress_yy + stress_zz * stress_zz + 2.0 * (stress_xy * stress_xy + stress_xz * stress_xz + stress_yz * stress_yz)
    shear_rate = 1.5 / (density * relax_zero) * jnp.sqrt(2.0 * contracted)
    viscosity = viscosity_limit + (viscosity_zero - viscosity_limit) * (1.0 + (carreau_time * shear_rate) ** 2) ** (0.5 * (carreau_power - 1.0))
    relax_time = 3.0 * viscosity + 0.5
    return populations - (populations - equilibrium) / relax_time

def pack_grains(own_grains, move_code, slot_cap):
    moving = move_code != 4
    region = jnp.where(move_code > 4, move_code - 1, move_code)
    matches = (move_code[None, :] == jnp.arange(9, dtype=jnp.int32)[:, None]).astype(jnp.int32)
    rank_of = lax.optimization_barrier(jnp.sum(matches * (jnp.cumsum(matches, axis=1, dtype=jnp.int32) - 1), axis=0, dtype=jnp.int32))
    target = region * slot_cap + rank_of
    placing = jnp.logical_and(target[:, None] == jnp.arange(8 * slot_cap, dtype=jnp.int32)[None, :], moving[:, None]).astype(jnp.float32)
    packed = jnp.dot(own_grains, placing, precision=lax.Precision.HIGHEST)
    kept_grains = own_grains * (move_code == 4).astype(jnp.float32)[None, :]
    return (kept_grains, packed)

def link_correction(cell_ids, direction_ids, picked, block_x, block_y):
    vel_table = jnp.asarray(velocity_cols)
    step_x = vel_table[:, 0][direction_ids]
    step_y = vel_table[:, 1][direction_ids]
    step_z = vel_table[:, 2][direction_ids]
    local_x = cell_ids // (E * Z)
    local_y = cell_ids // Z % E
    local_z = cell_ids % Z
    middle_x = (block_x * E + local_x).astype(jnp.float32) + 0.5 * step_x
    middle_y = (block_y * E + local_y).astype(jnp.float32) + 0.5 * step_y
    middle_z = local_z.astype(jnp.float32) + 0.5 * step_z
    rel_x = middle_x - picked[0]
    rel_y = middle_y - picked[1]
    rel_z = middle_z - picked[2]
    wall_x = picked[3] + picked[7] * rel_z - picked[8] * rel_y
    wall_y = picked[4] + picked[8] * rel_x - picked[6] * rel_z
    wall_z = picked[5] + picked[6] * rel_y - picked[7] * rel_x
    return 6.0 * jnp.asarray(lattice_wts)[direction_ids] * (step_x * wall_x + step_y * wall_y + step_z * wall_z)

def block_ranks(owners):
    count_blocks = owners.shape[-1]
    matching = owners[..., :, None] == owners[..., None, :]
    earlier = jnp.arange(count_blocks)[None, :] < jnp.arange(count_blocks)[:, None]
    return lax.optimization_barrier(jnp.sum(jnp.logical_and(matching, earlier).astype(jnp.int32), axis=-1, dtype=jnp.int32))

def set_values(row_values, target, values):
    return row_values.at[target].set(values)

def blockify(cells_grid):
    return cells_grid.reshape(Q, NBX, E, NBY, E, Z).transpose(1, 3, 0, 2, 4, 5).reshape(NBX, NBY, Q * CB)

def group_pack(own_grains, move_code):
    return pack_grains(own_grains, move_code, GCAP)

def reference(pdf, grains, grain_moves, owner_map, link_lists):
    grains_grid = grains.reshape(GV, GROUP, LANES, GR).transpose(1, 2, 0, 3)
    moves_grid = grain_moves.reshape(GROUP, LANES, GR)
    kept_grains, packed = jax.vmap(jax.vmap(group_pack))(grains_grid, moves_grid)
    regions = []
    for move_code in (0, 1, 2, 3, 5, 6, 7, 8):
        step_x = move_code // 3 - 1
        step_y = move_code % 3 - 1
        region = move_code if move_code < 4 else move_code - 1
        region_part = packed[:, :, :, region * GCAP:(region + 1) * GCAP]
        regions.append(jnp.roll(region_part, (step_x, step_y), axis=(0, 1)))
    grain_table = jnp.concatenate([kept_grains] + regions, axis=3).transpose(2, 0, 1, 3)
    new_grains = grain_table.reshape(GV, GROUP, LANES * GSLOT)
    slab_stack = jnp.moveaxis(pdf.reshape(Q, NBX, E * NY * Z), 1, 0)
    collided = jnp.moveaxis(lax.map(collide, slab_stack), 0, 1).reshape(Q, NX, NY, Z)
    passed = jnp.stack([jnp.roll(collided[direction], (int(lattice_vel[direction, 0]), int(lattice_vel[direction, 1]), int(lattice_vel[direction, 2])), axis=(0, 1, 2)) for direction in range(Q)])
    link_rows = link_lists.reshape(3, NBX, NBY, LB)
    cell_ids, direction_ids, grain_ids = (link_rows[0], link_rows[1], link_rows[2])
    column_x = jnp.arange(NBX, dtype=jnp.int32)[:, None, None]
    column_y = jnp.arange(NBY, dtype=jnp.int32)[None, :, None]
    picked = grain_table[:, column_x // BXD, column_y // BYD, grain_ids]
    correction = link_correction(cell_ids, direction_ids, picked, column_x, column_y)
    source = direction_ids * CB + cell_ids
    target = jnp.asarray(opposite_dir)[direction_ids] * CB + cell_ids
    star_blocks = blockify(collided)
    flow_blocks = blockify(passed)
    values = jnp.take_along_axis(star_blocks, source, axis=2) - correction
    final_blocks = jax.vmap(jax.vmap(set_values))(flow_blocks, target, values)
    owners = owner_map.reshape(GROUP, BXD, LANES, BYD).transpose(0, 2, 1, 3).reshape(GROUP, LANES, BLK)
    rank_of = block_ranks(owners)
    dest_row = owners * SLOTS + jnp.arange(GROUP, dtype=jnp.int32)[:, None, None] * CAPP + rank_of
    flat_dest = dest_row * LANES + jnp.arange(LANES, dtype=jnp.int32)[None, :, None]
    blocks_dev = final_blocks.reshape(GROUP, BXD, LANES, BYD, Q * CB).transpose(0, 2, 1, 3, 4).reshape(GROUP * LANES * BLK, Q * CB)
    total_blocks = GROUP * LANES * BLK
    source_of = jnp.full((GROUP * SLOTS * LANES,), total_blocks, jnp.int32).at[flat_dest.reshape(-1)].set(jnp.arange(total_blocks, dtype=jnp.int32))
    padded = jnp.concatenate([blocks_dev, jnp.zeros((1, Q * CB), blocks_dev.dtype)], axis=0)
    moved_blocks = padded[source_of].reshape(GROUP * SLOTS, LANES, Q, CB)
    return (moved_blocks, new_grains)
```

```python
import functools

import jax
import jax.numpy as jnp
import numpy as np
from jax import lax
from jax.experimental import pallas as pl
from jax.experimental.pallas import tpu as pltpu
from jax.sharding import PartitionSpec as P

MESH = pl.DeviceIdType.MESH
F32 = jnp.float32
BF16 = jnp.bfloat16

vel = [
    (0, 0, 0), (1, 0, 0), (-1, 0, 0), (0, 1, 0), (0, -1, 0), (0, 0, 1), (0, 0, -1),
    (1, 1, 0), (-1, -1, 0), (1, -1, 0), (-1, 1, 0),
    (1, 0, 1), (-1, 0, -1), (1, 0, -1), (-1, 0, 1),
    (0, 1, 1), (0, -1, -1), (0, 1, -1), (0, -1, 1),
]
opp = [0, 2, 1, 4, 3, 6, 5, 8, 7, 10, 9, 12, 11, 14, 13, 16, 15, 18, 17]
wts = [1.0 / 3.0] + [1.0 / 18.0] * 6 + [1.0 / 36.0] * 12
codes = (0, 1, 2, 3, 5, 6, 7, 8)
plus_x = [q for q in range(19) if vel[q][0] == 1]
minus_x = [q for q in range(19) if vel[q][0] == -1]
plus_y = [q for q in range(19) if vel[q][1] == 1]
minus_y = [q for q in range(19) if vel[q][1] == -1]
corner_dir = {(1, 1): 7, (-1, -1): 8, (1, -1): 9, (-1, 1): 10}


def steps_of(code):
    return code // 3 - 1, code % 3 - 1


def rows_of(code):
    dx, dy = steps_of(code)
    return 24 if dx == 0 else 16 if dy == 0 else 8


def roll(value, shift, axis):
    size = value.shape[axis]
    shift = shift % size
    return value if shift == 0 else pltpu.roll(value, shift, axis)


def split3(value):
    high = value.astype(BF16)
    rest = value - high.astype(F32)
    mid = rest.astype(BF16)
    low = (rest - mid.astype(F32)).astype(BF16)
    return high, mid, low


def collide(load):
    f = [load(q) for q in range(19)]
    sx = [f[q] for q in plus_x]
    density = functools.reduce(lambda a, b: a + b, f)

    def total(qs):
        return functools.reduce(lambda a, b: a + b, [f[q] for q in qs])

    px, mx = total(plus_x), total(minus_x)
    py, my = total(plus_y), total(minus_y)
    plus_z = [q for q in range(19) if vel[q][2] == 1]
    minus_z = [q for q in range(19) if vel[q][2] == -1]
    pz, mz = total(plus_z), total(minus_z)
    inverse = 1.0 / density
    ux, uy, uz = (px - mx) * inverse, (py - my) * inverse, (pz - mz) * inverse
    third = density * (1.0 / 3.0)
    dux, duy, duz = density * ux, density * uy, density * uz
    xx = (px + mx) - third - dux * ux
    yy = (py + my) - third - duy * uy
    zz = (pz + mz) - third - duz * uz
    xy = (f[7] + f[8]) - (f[9] + f[10]) - dux * uy
    xz = (f[11] + f[12]) - (f[13] + f[14]) - dux * uz
    yz = (f[15] + f[16]) - (f[17] + f[18]) - duy * uz
    contracted = xx * xx + yy * yy + zz * zz + 2.0 * (xy * xy + xz * xz + yz * yz)
    shear = (1.5 / 0.8) * inverse * jnp.sqrt(2.0 * contracted)
    scaled = 20.0 * shear
    viscosity = 0.01 + (0.1 - 0.01) * lax.rsqrt(jnp.sqrt(1.0 + scaled * scaled))
    omega = 1.0 / (3.0 * viscosity + 0.5)
    base = 1.0 - 1.5 * (ux * ux + uy * uy + uz * uz)
    keep = 1.0 - omega
    gain = {w: omega * density * w for w in set(wts)}
    out = []
    for q in range(19):
        c = None
        for step, u in zip(vel[q], (ux, uy, uz)):
            if step:
                term = u if step > 0 else -u
                c = term if c is None else c + term
        bracket = base if c is None else base + c * (3.0 + 4.5 * c)
        out.append(keep * f[q] + gain[wts[q]] * bracket)
    return out


def kernel(nx, ny, pdf_ref, grains_ref, moves_ref, owner_ref, links_ref,
           blocks_ref, table_ref,
           star, zstar, final, pad, tab, outbox, inbox, parcel,
           note_send, note_recv, block_send, block_recv, local_sem):
    gx = lax.axis_index("gx")
    gy = lax.axis_index("gy")

    def device(dx, dy):
        return (lax.rem(gx + dx + nx, nx), lax.rem(gy + dy + ny, ny))

    barrier = pltpu.get_barrier_semaphore()
    peers = [steps_of(m) for m in codes] + [(d, 0) for d in range(2, nx - 1)]
    for dx, dy in peers:
        pl.semaphore_signal(barrier, inc=1, device_id=device(dx, dy), device_id_type=MESH)

    lane = lax.broadcasted_iota(jnp.int32, (16, 128), 1)
    row = lax.broadcasted_iota(jnp.int32, (16, 128), 0)
    depth = lane % 8

    pad[...] = jnp.zeros_like(pad)
    own = grains_ref[:, 0, :]
    pad[0:26, :] = own
    code = moves_ref[...]
    kind = lax.broadcasted_iota(jnp.int32, (16, 256), 0)
    match = jnp.where(kind == code, 1.0, 0.0)
    before = jnp.where(
        lax.broadcasted_iota(jnp.int32, (256, 256), 0)
        < lax.broadcasted_iota(jnp.int32, (256, 256), 1), 1.0, 0.0)
    counts = jnp.dot(match.astype(BF16), before.astype(BF16), preferred_element_type=F32)
    rank = jnp.sum(match * counts, axis=0, keepdims=True).astype(jnp.int32)
    region = jnp.where(code > 4, code - 1, code)
    target = jnp.where(code == 4, -1, region * 8 + rank)
    slot = lax.broadcasted_iota(jnp.int32, (64, 256), 0)
    placing = jnp.where(slot == target, 1.0, 0.0).astype(BF16)
    parts = jnp.concatenate(list(split3(pad[...])) + [jnp.zeros((32, 256), BF16)], axis=0)
    packed = lax.dot_general(placing, parts, (((1,), (1,)), ((), ())),
                             preferred_element_type=F32)
    packed = packed + roll(packed, -32, 1) + roll(packed, -64, 1)
    packed = jnp.where(lax.broadcasted_iota(jnp.int32, (64, 128), 1) < 32, packed, 0.0)

    collided = collide(lambda q: pdf_ref[q])
    for q in range(19):
        star[q] = collided[q]
        shifted = collided[q]
        if vel[q][2] == 1:
            shifted = jnp.where(depth == 0, roll(shifted, -7, 1), roll(shifted, 1, 1))
        elif vel[q][2] == -1:
            shifted = jnp.where(depth == 7, roll(shifted, 7, 1), roll(shifted, -1, 1))
        zstar[q] = shifted

    for k, m in enumerate(codes):
        dx, dy = steps_of(m)
        tile = packed[k * 8:(k + 1) * 8, :]
        if dx and dy:
            edge = zstar[corner_dir[dx, dy], pl.ds(15 if dx == 1 else 0, 1), :]
            if dy == -1:
                edge = roll(jnp.broadcast_to(edge, (8, 128)), 120, 1)
            tile = jnp.where(lane[0:8] >= 120, edge, tile)
        outbox[k, 0:8, :] = tile
        if dy == 0:
            for i, q in enumerate(plus_x if dx == 1 else minus_x):
                outbox[k, 8 + i:9 + i, :] = zstar[q, pl.ds(15 if dx == 1 else 0, 1), :]
        elif dx == 0:
            face = jnp.zeros((16, 128), F32)
            for i, q in enumerate(plus_y if dy == 1 else minus_y):
                moved = roll(zstar[q], 8 * i + (8 if dy == 1 else 0), 1)
                face = jnp.where(lane // 8 == i, moved, face)
            outbox[k, 8:24, :] = face

    pl.semaphore_wait(barrier, len(peers))
    notes = []
    for k, m in enumerate(codes):
        copy = pltpu.make_async_remote_copy(
            src_ref=outbox.at[k, pl.ds(0, rows_of(m))],
            dst_ref=inbox.at[k, pl.ds(0, rows_of(m))],
            send_sem=note_send.at[k], recv_sem=note_recv.at[k],
            device_id=device(*steps_of(m)), device_id_type=MESH)
        copy.start()
        notes.append(copy)

    kept = own * jnp.where(code == 4, 1.0, 0.0)
    tab[...] = jnp.zeros_like(tab)
    tab[0:26, 0:256] = kept
    cells, dirs, slots = links_ref[0], links_ref[1], links_ref[2]

    def step_along(axis):
        value = jnp.zeros((2, 512), F32)
        for q in range(1, 19):
            if vel[q][axis]:
                value = jnp.where(dirs == q, float(vel[q][axis]), value)
        return value

    step_x, step_y, step_z = step_along(0), step_along(1), step_along(2)
    half = lax.broadcasted_iota(jnp.int32, (2, 512), 1) // 256
    bx = lax.broadcasted_iota(jnp.int32, (2, 512), 0)
    cell_x, cell_y, cell_z = cells // 64, cells // 8 % 8, cells % 8
    mid_x = ((gx * 2 + bx) * 8 + cell_x).astype(F32) + 0.5 * step_x
    mid_y = ((gy * 2 + half) * 8 + cell_y).astype(F32) + 0.5 * step_y
    mid_z = cell_z.astype(F32) + 0.5 * step_z
    scale = jnp.where(dirs < 7, 6.0 / 18.0, 6.0 / 36.0)
    place = half * 64 + cells % 64
    fdirs = dirs.astype(F32)

    for copy in notes:
        copy.wait()

    incoming = inbox[:, 0:8, :].reshape(64, 128)
    incoming = jnp.concatenate([incoming, jnp.zeros((64, 128), F32)], axis=0).T
    tab[0:26, 256:384] = incoming[0:26, :]
    table_ref[...] = tab[0:26, 0:320]
    features = jnp.concatenate(list(split3(tab[0:16, :])), axis=0)
    dense = []
    for b in range(2):
        def at(value):
            return value[b:b + 1, :]

        chosen = jnp.where(
            lax.broadcasted_iota(jnp.int32, (384, 512), 0) == at(slots), 1.0, 0.0).astype(BF16)
        g = jnp.dot(features, chosen, preferred_element_type=F32)
        g = g[0:16] + g[16:32] + g[32:48]
        rel_x, rel_y, rel_z = at(mid_x) - g[0:1], at(mid_y) - g[1:2], at(mid_z) - g[2:3]
        wall_x = g[3:4] + g[7:8] * rel_z - g[8:9] * rel_y
        wall_y = g[4:5] + g[8:9] * rel_x - g[6:7] * rel_z
        wall_z = g[5:6] + g[6:7] * rel_y - g[7:8] * rel_x
        correction = at(scale) * (
            at(step_x) * wall_x + at(step_y) * wall_y + at(step_z) * wall_z)
        in_row = lax.broadcasted_iota(jnp.int32, (8, 512), 0) == at(cell_x)
        values = [p.astype(F32) for p in split3(correction)] + [at(fdirs)]
        spread = jnp.concatenate(
            [jnp.where(in_row, value, 0.0) for value in values], axis=0).astype(BF16)
        where_to = jnp.where(
            lax.broadcasted_iota(jnp.int32, (128, 512), 0) == at(place), 1.0, 0.0).astype(BF16)
        dense.append(lax.dot_general(spread, where_to, (((1,), (1,)), ((), ())),
                                     preferred_element_type=F32))
    correction = jnp.concatenate([d[0:8] + d[8:16] + d[16:24] for d in dense], axis=0)
    link_dir = jnp.concatenate([d[24:32] for d in dense], axis=0)

    region_of = {steps_of(m): k for k, m in enumerate(codes)}
    for q in range(19):
        sx, sy, _ = vel[q]
        value = zstar[q]
        edge_lane = lane < 8 if sy == 1 else lane >= 120
        if sy:
            i = (plus_y if sy == 1 else minus_y).index(q)
            ghost = inbox[region_of[0, sy], 8:24, :]
            ghost = roll(ghost, -8 * i + (0 if sy == 1 else 120), 1)
            value = jnp.where(edge_lane, ghost, roll(value, 8 * sy, 1))
        if sx:
            i = (plus_x if sx == 1 else minus_x).index(q)
            line = inbox[region_of[sx, 0], 8 + i:9 + i, :]
            if sy:
                line = roll(jnp.broadcast_to(line, (8, 128)), 8 * sy, 1)
                corner = inbox[region_of[sx, sy], 0:8, :]
                corner = roll(corner, 8, 1) if sy == 1 else corner
                line = jnp.where(edge_lane[0:8], corner, line)[0:1]
            value = jnp.where(row == (0 if sx == 1 else 15), line, roll(value, sx, 0))
        if q:
            value = jnp.where(link_dir == float(opp[q]), star[opp[q]] - correction, value)
        final[q * 16:(q + 1) * 16, :] = value

    wide = lax.broadcasted_iota(jnp.int32, (24, 128), 1) < 64
    holds = [jnp.full((24, 128), owner_ref[n // 2, n % 2], jnp.int32) for n in range(4)]
    for k in range(4):
        pieces = []
        for b in range(2):
            first = final[pl.ds(b * 8 + 2 * k, 24, stride=16), :]
            second = final[pl.ds(b * 8 + 2 * k + 1, 24, stride=16), :]
            pieces.append(jnp.where(wide, first, roll(second, 64, 1)))
            pieces.append(jnp.where(wide, roll(first, 64, 1), second))
        for o in range(nx):
            value = jnp.zeros((24, 128), F32)
            for n in range(4):
                value = jnp.where(holds[n] == o, pieces[n], value)
            parcel[o, :, k * 128:(k + 1) * 128] = value[0:19]

    sends = []
    for d in range(1, nx):
        to = lax.rem(gx + d, nx)
        copy = pltpu.make_async_remote_copy(
            src_ref=parcel.at[to], dst_ref=blocks_ref.at[gx],
            send_sem=block_send.at[d - 1], recv_sem=block_recv.at[d - 1],
            device_id=(to, gy), device_id_type=MESH)
        copy.start()
        sends.append(copy)
    here = pltpu.make_async_copy(parcel.at[gx], blocks_ref.at[gx], local_sem)
    here.start()
    here.wait()
    for copy in sends:
        copy.wait()


def body(pdf, grains, grain_moves, owner_map, link_lists):
    nx, ny = lax.axis_size("gx"), lax.axis_size("gy")
    vmem = pl.BlockSpec(memory_space=pltpu.VMEM)
    blocks, table = pl.pallas_call(
        functools.partial(kernel, nx, ny),
        out_shape=(jax.ShapeDtypeStruct((nx, 19, 512), F32),
                   jax.ShapeDtypeStruct((26, 320), F32)),
        in_specs=[vmem, vmem, vmem, pl.BlockSpec(memory_space=pltpu.SMEM), vmem],
        out_specs=(pl.BlockSpec(memory_space=pl.ANY), vmem),
        scratch_shapes=[
            pltpu.VMEM((19, 16, 128), F32),
            pltpu.VMEM((19, 16, 128), F32),
            pltpu.VMEM((384, 128), F32),
            pltpu.VMEM((32, 256), F32),
            pltpu.VMEM((32, 384), F32),
            pltpu.VMEM((8, 24, 128), F32),
            pltpu.VMEM((8, 24, 128), F32),
            pltpu.VMEM((nx, 19, 512), F32),
            pltpu.SemaphoreType.DMA((8,)),
            pltpu.SemaphoreType.DMA((8,)),
            pltpu.SemaphoreType.DMA((nx - 1,)),
            pltpu.SemaphoreType.DMA((nx - 1,)),
            pltpu.SemaphoreType.DMA,
        ],
        compiler_params=pltpu.CompilerParams(
            collective_id=0, has_side_effects=True, vmem_limit_bytes=32 * 1024 * 1024),
        name="slab_step",
    )(pdf, grains, grain_moves, owner_map, link_lists)
    return blocks[:, None], table[:, None, :]


def solution(mesh):
    in_specs = (
        P(None, "gx", "gy"),
        P(None, "gx", "gy"),
        P("gx", "gy"),
        P("gx", "gy"),
        P(None, "gx", "gy"),
    )
    out_specs = (P("gx", "gy", None, None), P(None, "gx", "gy"))
    return jax.shard_map(body, mesh=mesh, in_specs=in_specs, out_specs=out_specs, check_vma=False)
```

```python
import functools

import jax
import jax.numpy as jnp
import numpy as np
from jax import lax
from jax.experimental import pallas as pl
from jax.experimental.pallas import tpu as pltpu
from jax.sharding import PartitionSpec as P

MESH = pl.DeviceIdType.MESH
F32 = jnp.float32
BF16 = jnp.bfloat16

vel = [
    (0, 0, 0), (1, 0, 0), (-1, 0, 0), (0, 1, 0), (0, -1, 0), (0, 0, 1), (0, 0, -1),
    (1, 1, 0), (-1, -1, 0), (1, -1, 0), (-1, 1, 0),
    (1, 0, 1), (-1, 0, -1), (1, 0, -1), (-1, 0, 1),
    (0, 1, 1), (0, -1, -1), (0, 1, -1), (0, -1, 1),
]
opp = [0, 2, 1, 4, 3, 6, 5, 8, 7, 10, 9, 12, 11, 14, 13, 16, 15, 18, 17]
wts = [1.0 / 3.0] + [1.0 / 18.0] * 6 + [1.0 / 36.0] * 12
codes = (0, 1, 2, 3, 5, 6, 7, 8)
plus_x = [q for q in range(19) if vel[q][0] == 1]
minus_x = [q for q in range(19) if vel[q][0] == -1]
plus_y = [q for q in range(19) if vel[q][1] == 1]
minus_y = [q for q in range(19) if vel[q][1] == -1]
corner_dir = {(1, 1): 7, (-1, -1): 8, (1, -1): 9, (-1, 1): 10}


def steps_of(code):
    return code // 3 - 1, code % 3 - 1


def rows_of(code):
    dx, dy = steps_of(code)
    return 24 if dx == 0 else 16 if dy == 0 else 8


def roll(value, shift, axis):
    size = value.shape[axis]
    shift = shift % size
    return value if shift == 0 else pltpu.roll(value, shift, axis)


def split3(value):
    high = value.astype(BF16)
    rest = value - high.astype(F32)
    mid = rest.astype(BF16)
    low = (rest - mid.astype(F32)).astype(BF16)
    return high, mid, low


def collide(load):
    f = [load(q) for q in range(19)]
    sx = [f[q] for q in plus_x]
    density = functools.reduce(lambda a, b: a + b, f)

    def total(qs):
        return functools.reduce(lambda a, b: a + b, [f[q] for q in qs])

    px, mx = total(plus_x), total(minus_x)
    py, my = total(plus_y), total(minus_y)
    plus_z = [q for q in range(19) if vel[q][2] == 1]
    minus_z = [q for q in range(19) if vel[q][2] == -1]
    pz, mz = total(plus_z), total(minus_z)
    inverse = 1.0 / density
    ux, uy, uz = (px - mx) * inverse, (py - my) * inverse, (pz - mz) * inverse
    third = density * (1.0 / 3.0)
    dux, duy, duz = density * ux, density * uy, density * uz
    xx = (px + mx) - third - dux * ux
    yy = (py + my) - third - duy * uy
    zz = (pz + mz) - third - duz * uz
    xy = (f[7] + f[8]) - (f[9] + f[10]) - dux * uy
    xz = (f[11] + f[12]) - (f[13] + f[14]) - dux * uz
    yz = (f[15] + f[16]) - (f[17] + f[18]) - duy * uz
    contracted = xx * xx + yy * yy + zz * zz + 2.0 * (xy * xy + xz * xz + yz * yz)
    shear = (1.5 / 0.8) * inverse * jnp.sqrt(2.0 * contracted)
    scaled = 20.0 * shear
    viscosity = 0.01 + (0.1 - 0.01) * lax.rsqrt(jnp.sqrt(1.0 + scaled * scaled))
    omega = 1.0 / (3.0 * viscosity + 0.5)
    base = 1.0 - 1.5 * (ux * ux + uy * uy + uz * uz)
    keep = 1.0 - omega
    gain = {w: omega * density * w for w in set(wts)}
    out = []
    for q in range(19):
        c = None
        for step, u in zip(vel[q], (ux, uy, uz)):
            if step:
                term = u if step > 0 else -u
                c = term if c is None else c + term
        bracket = base if c is None else base + c * (3.0 + 4.5 * c)
        out.append(keep * f[q] + gain[wts[q]] * bracket)
    return out


def kernel(nx, ny, pdf_hbm, grains_hbm, moves_hbm, owner_hbm, links_hbm,
           blocks_ref, table_ref,
           pdf_ref, grains_ref, moves_ref, owner_ref, links_ref, load_sem, star, zstar, final, pad, tab, outbox, inbox, parcel,
           note_send, note_recv, block_send, block_recv, local_sem):
    gx = lax.axis_index("gx")
    gy = lax.axis_index("gy")

    def device(dx, dy):
        return (lax.rem(gx + dx + nx, nx), lax.rem(gy + dy + ny, ny))

    loads = [
        pltpu.make_async_copy(source, held, load_sem.at[i])
        for i, (source, held) in enumerate((
            (grains_hbm, grains_ref), (moves_hbm, moves_ref), (pdf_hbm, pdf_ref),
            (owner_hbm, owner_ref), (links_hbm, links_ref)))
    ]
    for load in loads:
        load.start()
    barrier = pltpu.get_barrier_semaphore()
    peers = [steps_of(m) for m in codes] + [(d, 0) for d in range(2, nx - 1)]
    for dx, dy in peers:
        pl.semaphore_signal(barrier, inc=1, device_id=device(dx, dy), device_id_type=MESH)

    lane = lax.broadcasted_iota(jnp.int32, (16, 128), 1)
    row = lax.broadcasted_iota(jnp.int32, (16, 128), 0)
    depth = lane % 8

    pad[...] = jnp.zeros_like(pad)
    for load in loads:
        load.wait()
    own = grains_ref[:, 0, :]
    pad[0:26, :] = own
    code = moves_ref[...]
    kind = lax.broadcasted_iota(jnp.int32, (16, 256), 0)
    match = jnp.where(kind == code, 1.0, 0.0)
    before = jnp.where(
        lax.broadcasted_iota(jnp.int32, (256, 256), 0)
        < lax.broadcasted_iota(jnp.int32, (256, 256), 1), 1.0, 0.0)
    counts = jnp.dot(match.astype(BF16), before.astype(BF16), preferred_element_type=F32)
    rank = jnp.sum(match * counts, axis=0, keepdims=True).astype(jnp.int32)
    region = jnp.where(code > 4, code - 1, code)
    target = jnp.where(code == 4, -1, region * 8 + rank)
    slot = lax.broadcasted_iota(jnp.int32, (64, 256), 0)
    placing = jnp.where(slot == target, 1.0, 0.0).astype(BF16)
    parts = jnp.concatenate(list(split3(pad[...])) + [jnp.zeros((32, 256), BF16)], axis=0)
    packed = lax.dot_general(placing, parts, (((1,), (1,)), ((), ())),
                             preferred_element_type=F32)
    packed = packed + roll(packed, -32, 1) + roll(packed, -64, 1)
    packed = jnp.where(lax.broadcasted_iota(jnp.int32, (64, 128), 1) < 32, packed, 0.0)

    collided = collide(lambda q: pdf_ref[q])
    for q in range(19):
        star[q] = collided[q]
        shifted = collided[q]
        if vel[q][2] == 1:
            shifted = jnp.where(depth == 0, roll(shifted, -7, 1), roll(shifted, 1, 1))
        elif vel[q][2] == -1:
            shifted = jnp.where(depth == 7, roll(shifted, 7, 1), roll(shifted, -1, 1))
        zstar[q] = shifted

    for k, m in enumerate(codes):
        dx, dy = steps_of(m)
        tile = packed[k * 8:(k + 1) * 8, :]
        if dx and dy:
            edge = zstar[corner_dir[dx, dy], pl.ds(15 if dx == 1 else 0, 1), :]
            if dy == -1:
                edge = roll(jnp.broadcast_to(edge, (8, 128)), 120, 1)
            tile = jnp.where(lane[0:8] >= 120, edge, tile)
        outbox[k, 0:8, :] = tile
        if dy == 0:
            for i, q in enumerate(plus_x if dx == 1 else minus_x):
                outbox[k, 8 + i:9 + i, :] = zstar[q, pl.ds(15 if dx == 1 else 0, 1), :]
        elif dx == 0:
            face = jnp.zeros((16, 128), F32)
            for i, q in enumerate(plus_y if dy == 1 else minus_y):
                moved = roll(zstar[q], 8 * i + (8 if dy == 1 else 0), 1)
                face = jnp.where(lane // 8 == i, moved, face)
            outbox[k, 8:24, :] = face

    pl.semaphore_wait(barrier, len(peers))
    notes = []
    for k, m in enumerate(codes):
        copy = pltpu.make_async_remote_copy(
            src_ref=outbox.at[k, pl.ds(0, rows_of(m))],
            dst_ref=inbox.at[k, pl.ds(0, rows_of(m))],
            send_sem=note_send.at[k], recv_sem=note_recv.at[k],
            device_id=device(*steps_of(m)), device_id_type=MESH)
        copy.start()
        notes.append(copy)

    kept = own * jnp.where(code == 4, 1.0, 0.0)
    tab[...] = jnp.zeros_like(tab)
    tab[0:26, 0:256] = kept
    cells, dirs, slots = links_ref[0], links_ref[1], links_ref[2]

    def step_along(axis):
        value = jnp.zeros((2, 512), F32)
        for q in range(1, 19):
            if vel[q][axis]:
                value = jnp.where(dirs == q, float(vel[q][axis]), value)
        return value

    step_x, step_y, step_z = step_along(0), step_along(1), step_along(2)
    half = lax.broadcasted_iota(jnp.int32, (2, 512), 1) // 256
    bx = lax.broadcasted_iota(jnp.int32, (2, 512), 0)
    cell_x, cell_y, cell_z = cells // 64, cells // 8 % 8, cells % 8
    mid_x = ((gx * 2 + bx) * 8 + cell_x).astype(F32) + 0.5 * step_x
    mid_y = ((gy * 2 + half) * 8 + cell_y).astype(F32) + 0.5 * step_y
    mid_z = cell_z.astype(F32) + 0.5 * step_z
    scale = jnp.where(dirs < 7, 6.0 / 18.0, 6.0 / 36.0)
    place = half * 64 + cells % 64
    fdirs = dirs.astype(F32)

    features = jnp.concatenate(list(split3(tab[0:16, 0:256])), axis=0)
    resting, arriving, targets = [], [], []
    for b in range(2):
        slot = slots[b:b + 1, :]
        chosen = jnp.where(
            lax.broadcasted_iota(jnp.int32, (256, 512), 0) == slot, 1.0, 0.0).astype(BF16)
        resting.append(jnp.dot(features, chosen, preferred_element_type=F32))
        arriving.append(jnp.where(
            lax.broadcasted_iota(jnp.int32, (128, 512), 0) + 256 == slot,
            1.0, 0.0).astype(BF16))
        targets.append(jnp.where(
            lax.broadcasted_iota(jnp.int32, (128, 512), 0) == place[b:b + 1, :],
            1.0, 0.0).astype(BF16))

    for q in range(19):
        sx, sy, _ = vel[q]
        if sx or sy:
            zstar[q] = roll(roll(zstar[q], 8 * sy, 1), sx, 0)

    for copy in notes:
        copy.wait_recv()

    incoming = inbox[:, 0:8, :].reshape(64, 128)
    incoming = jnp.concatenate([incoming, jnp.zeros((64, 128), F32)], axis=0).T
    tab[0:26, 256:384] = incoming[0:26, :]
    table_ref[...] = tab[0:26, 0:320]
    features = jnp.concatenate(list(split3(tab[0:16, 256:384])), axis=0)
    dense = []
    for b in range(2):
        def at(value):
            return value[b:b + 1, :]

        g = resting[b] + jnp.dot(features, arriving[b], preferred_element_type=F32)
        g = g[0:16] + g[16:32] + g[32:48]
        rel_x, rel_y, rel_z = at(mid_x) - g[0:1], at(mid_y) - g[1:2], at(mid_z) - g[2:3]
        wall_x = g[3:4] + g[7:8] * rel_z - g[8:9] * rel_y
        wall_y = g[4:5] + g[8:9] * rel_x - g[6:7] * rel_z
        wall_z = g[5:6] + g[6:7] * rel_y - g[7:8] * rel_x
        correction = at(scale) * (
            at(step_x) * wall_x + at(step_y) * wall_y + at(step_z) * wall_z)
        in_row = lax.broadcasted_iota(jnp.int32, (8, 512), 0) == at(cell_x)
        values = [p.astype(F32) for p in split3(correction)] + [at(fdirs)]
        spread = jnp.concatenate(
            [jnp.where(in_row, value, 0.0) for value in values], axis=0).astype(BF16)
        dense.append(lax.dot_general(spread, targets[b], (((1,), (1,)), ((), ())),
                                     preferred_element_type=F32))
    correction = jnp.concatenate([d[0:8] + d[8:16] + d[16:24] for d in dense], axis=0)
    link_dir = jnp.concatenate([d[24:32] for d in dense], axis=0)

    region_of = {steps_of(m): k for k, m in enumerate(codes)}
    for q in range(19):
        sx, sy, _ = vel[q]
        value = zstar[q]
        edge_lane = lane < 8 if sy == 1 else lane >= 120
        if sy:
            i = (plus_y if sy == 1 else minus_y).index(q)
            ghost = inbox[region_of[0, sy], 8:24, :]
            ghost = roll(ghost, -8 * i + (0 if sy == 1 else 120), 1)
            value = jnp.where(edge_lane, roll(ghost, sx, 0), value)
        if sx:
            i = (plus_x if sx == 1 else minus_x).index(q)
            line = inbox[region_of[sx, 0], 8 + i:9 + i, :]
            if sy:
                line = roll(jnp.broadcast_to(line, (8, 128)), 8 * sy, 1)
                corner = inbox[region_of[sx, sy], 0:8, :]
                corner = roll(corner, 8, 1) if sy == 1 else corner
                line = jnp.where(edge_lane[0:8], corner, line)[0:1]
            value = jnp.where(row == (0 if sx == 1 else 15), line, value)
        if q:
            value = jnp.where(link_dir == float(opp[q]), star[opp[q]] - correction, value)
        final[q * 16:(q + 1) * 16, :] = value

    wide = lax.broadcasted_iota(jnp.int32, (24, 128), 1) < 64
    holds = [jnp.broadcast_to(owner_ref[n // 2:n // 2 + 1, n % 2:n % 2 + 1], (24, 128))
             for n in range(4)]
    pieces = []
    for k in range(4):
        for b in range(2):
            first = final[pl.ds(b * 8 + 2 * k, 24, stride=16), :]
            second = final[pl.ds(b * 8 + 2 * k + 1, 24, stride=16), :]
            pieces.append(jnp.where(wide, first, roll(second, 64, 1)))
            pieces.append(jnp.where(wide, roll(first, 64, 1), second))
    sends = []
    for d in list(range(1, nx)) + [0]:
        to = lax.rem(gx + d, nx)
        here = [hold == to for hold in holds]
        for k in range(4):
            value = jnp.zeros((24, 128), F32)
            for n in range(4):
                value = jnp.where(here[n], pieces[4 * k + n], value)
            parcel[d, :, k * 128:(k + 1) * 128] = value[0:19]
        if d:
            copy = pltpu.make_async_remote_copy(
                src_ref=parcel.at[d], dst_ref=blocks_ref.at[gx],
                send_sem=block_send.at[d - 1], recv_sem=block_recv.at[d - 1],
                device_id=(to, gy), device_id_type=MESH)
        else:
            copy = pltpu.make_async_copy(parcel.at[0], blocks_ref.at[gx], local_sem)
        copy.start()
        sends.append(copy)
    for copy in notes:
        copy.wait_send()
    for copy in sends:
        copy.wait()


def body(pdf, grains, grain_moves, owner_map, link_lists):
    nx, ny = lax.axis_size("gx"), lax.axis_size("gy")
    vmem = pl.BlockSpec(memory_space=pltpu.VMEM)
    blocks, table = pl.pallas_call(
        functools.partial(kernel, nx, ny),
        out_shape=(jax.ShapeDtypeStruct((nx, 19, 512), F32),
                   jax.ShapeDtypeStruct((26, 320), F32)),
        in_specs=[pl.BlockSpec(memory_space=pltpu.HBM)] * 5,
        out_specs=(pl.BlockSpec(memory_space=pl.ANY), vmem),
        scratch_shapes=[
            pltpu.VMEM(pdf.shape, F32),
            pltpu.VMEM(grains.shape, F32),
            pltpu.VMEM(grain_moves.shape, jnp.int32),
            pltpu.VMEM(owner_map.shape, jnp.int32),
            pltpu.VMEM(link_lists.shape, jnp.int32),
            pltpu.SemaphoreType.DMA((5,)),
            pltpu.VMEM((19, 16, 128), F32),
            pltpu.VMEM((19, 16, 128), F32),
            pltpu.VMEM((384, 128), F32),
            pltpu.VMEM((32, 256), F32),
            pltpu.VMEM((32, 384), F32),
            pltpu.VMEM((8, 24, 128), F32),
            pltpu.VMEM((8, 24, 128), F32),
            pltpu.VMEM((nx, 19, 512), F32),
            pltpu.SemaphoreType.DMA((8,)),
            pltpu.SemaphoreType.DMA((8,)),
            pltpu.SemaphoreType.DMA((nx - 1,)),
            pltpu.SemaphoreType.DMA((nx - 1,)),
            pltpu.SemaphoreType.DMA,
        ],
        compiler_params=pltpu.CompilerParams(
            collective_id=0, has_side_effects=True, vmem_limit_bytes=32 * 1024 * 1024),
        name="slab_step",
    )(pdf, grains, grain_moves, owner_map, link_lists)
    return blocks[:, None], table[:, None, :]


def solution(mesh):
    in_specs = (
        P(None, "gx", "gy"),
        P(None, "gx", "gy"),
        P("gx", "gy"),
        P("gx", "gy"),
        P(None, "gx", "gy"),
    )
    out_specs = (P("gx", "gy", None, None), P(None, "gx", "gy"))
    return jax.shard_map(body, mesh=mesh, in_specs=in_specs, out_specs=out_specs, check_vma=False)
```

```python
import functools

import jax
import jax.numpy as jnp
import numpy as np
from jax import lax
from jax.experimental import pallas as pl
from jax.experimental.pallas import tpu as pltpu
from jax.sharding import PartitionSpec as P

MESH = pl.DeviceIdType.MESH
F32 = jnp.float32
BF16 = jnp.bfloat16

vel = [
    (0, 0, 0), (1, 0, 0), (-1, 0, 0), (0, 1, 0), (0, -1, 0), (0, 0, 1), (0, 0, -1),
    (1, 1, 0), (-1, -1, 0), (1, -1, 0), (-1, 1, 0),
    (1, 0, 1), (-1, 0, -1), (1, 0, -1), (-1, 0, 1),
    (0, 1, 1), (0, -1, -1), (0, 1, -1), (0, -1, 1),
]
opp = [0, 2, 1, 4, 3, 6, 5, 8, 7, 10, 9, 12, 11, 14, 13, 16, 15, 18, 17]
wts = [1.0 / 3.0] + [1.0 / 18.0] * 6 + [1.0 / 36.0] * 12
codes = (0, 1, 2, 3, 5, 6, 7, 8)
plus_x = [q for q in range(19) if vel[q][0] == 1]
minus_x = [q for q in range(19) if vel[q][0] == -1]
plus_y = [q for q in range(19) if vel[q][1] == 1]
minus_y = [q for q in range(19) if vel[q][1] == -1]
corner_dir = {(1, 1): 7, (-1, -1): 8, (1, -1): 9, (-1, 1): 10}


def steps_of(code):
    return code // 3 - 1, code % 3 - 1


def rows_of(code):
    dx, dy = steps_of(code)
    return 24 if dx == 0 else 16 if dy == 0 else 8


def roll(value, shift, axis):
    size = value.shape[axis]
    shift = shift % size
    return value if shift == 0 else pltpu.roll(value, shift, axis)


def split3(value):
    high = value.astype(BF16)
    rest = value - high.astype(F32)
    mid = rest.astype(BF16)
    low = (rest - mid.astype(F32)).astype(BF16)
    return high, mid, low


def collide(load):
    f = [load(q) for q in range(19)]
    sx = [f[q] for q in plus_x]
    density = functools.reduce(lambda a, b: a + b, f)

    def total(qs):
        return functools.reduce(lambda a, b: a + b, [f[q] for q in qs])

    px, mx = total(plus_x), total(minus_x)
    py, my = total(plus_y), total(minus_y)
    plus_z = [q for q in range(19) if vel[q][2] == 1]
    minus_z = [q for q in range(19) if vel[q][2] == -1]
    pz, mz = total(plus_z), total(minus_z)
    inverse = 1.0 / density
    ux, uy, uz = (px - mx) * inverse, (py - my) * inverse, (pz - mz) * inverse
    third = density * (1.0 / 3.0)
    dux, duy, duz = density * ux, density * uy, density * uz
    xx = (px + mx) - third - dux * ux
    yy = (py + my) - third - duy * uy
    zz = (pz + mz) - third - duz * uz
    xy = (f[7] + f[8]) - (f[9] + f[10]) - dux * uy
    xz = (f[11] + f[12]) - (f[13] + f[14]) - dux * uz
    yz = (f[15] + f[16]) - (f[17] + f[18]) - duy * uz
    contracted = xx * xx + yy * yy + zz * zz + 2.0 * (xy * xy + xz * xz + yz * yz)
    shear = (1.5 / 0.8) * inverse * jnp.sqrt(2.0 * contracted)
    scaled = 20.0 * shear
    viscosity = 0.01 + (0.1 - 0.01) * lax.rsqrt(jnp.sqrt(1.0 + scaled * scaled))
    omega = 1.0 / (3.0 * viscosity + 0.5)
    base = 1.0 - 1.5 * (ux * ux + uy * uy + uz * uz)
    keep = 1.0 - omega
    gain = {w: omega * density * w for w in set(wts)}
    out = []
    for q in range(19):
        c = None
        for step, u in zip(vel[q], (ux, uy, uz)):
            if step:
                term = u if step > 0 else -u
                c = term if c is None else c + term
        bracket = base if c is None else base + c * (3.0 + 4.5 * c)
        out.append(keep * f[q] + gain[wts[q]] * bracket)
    return out


def kernel(nx, ny, pdf_hbm, grains_hbm, moves_hbm, owner_hbm, links_hbm,
           blocks_ref, table_ref,
           pdf_ref, grains_ref, moves_ref, owner_ref, links_ref, load_sem, star, zstar, final, pad, tab, outbox, inbox, parcel,
           note_send, note_recv, block_send, block_recv, local_sem):
    gx = lax.axis_index("gx")
    gy = lax.axis_index("gy")

    def device(dx, dy):
        return (lax.rem(gx + dx + nx, nx), lax.rem(gy + dy + ny, ny))

    loads = [
        pltpu.make_async_copy(source, held, load_sem.at[i])
        for i, (source, held) in enumerate((
            (grains_hbm, grains_ref), (moves_hbm, moves_ref), (pdf_hbm, pdf_ref),
            (owner_hbm, owner_ref), (links_hbm, links_ref)))
    ]
    for load in loads:
        load.start()
    barrier = pltpu.get_barrier_semaphore()
    peers = [steps_of(m) for m in codes] + [(d, 0) for d in range(2, nx - 1)]
    for dx, dy in peers:
        pl.semaphore_signal(barrier, inc=1, device_id=device(dx, dy), device_id_type=MESH)

    lane = lax.broadcasted_iota(jnp.int32, (16, 128), 1)
    row = lax.broadcasted_iota(jnp.int32, (16, 128), 0)
    depth = lane % 8

    pad[...] = jnp.zeros_like(pad)
    for load in loads:
        load.wait()
    own = grains_ref[:, 0, :]
    pad[0:26, :] = own
    code = moves_ref[...]
    kind = lax.broadcasted_iota(jnp.int32, (16, 256), 0)
    match = jnp.where(kind == code, 1.0, 0.0)
    before = jnp.where(
        lax.broadcasted_iota(jnp.int32, (256, 256), 0)
        < lax.broadcasted_iota(jnp.int32, (256, 256), 1), 1.0, 0.0)
    counts = jnp.dot(match.astype(BF16), before.astype(BF16), preferred_element_type=F32)
    rank = jnp.sum(match * counts, axis=0, keepdims=True).astype(jnp.int32)
    region = jnp.where(code > 4, code - 1, code)
    target = jnp.where(code == 4, -1, region * 8 + rank)
    slot = lax.broadcasted_iota(jnp.int32, (64, 256), 0)
    placing = jnp.where(slot == target, 1.0, 0.0).astype(BF16)
    parts = jnp.concatenate(list(split3(pad[...])) + [jnp.zeros((32, 256), BF16)], axis=0)
    packed = lax.dot_general(placing, parts, (((1,), (1,)), ((), ())),
                             preferred_element_type=F32)
    packed = packed + roll(packed, -32, 1) + roll(packed, -64, 1)
    packed = jnp.where(lax.broadcasted_iota(jnp.int32, (64, 128), 1) < 32, packed, 0.0)

    collided = collide(lambda q: pdf_ref[q])
    for q in range(19):
        star[q] = collided[q]
        shifted = collided[q]
        if vel[q][2] == 1:
            shifted = jnp.where(depth == 0, roll(shifted, -7, 1), roll(shifted, 1, 1))
        elif vel[q][2] == -1:
            shifted = jnp.where(depth == 7, roll(shifted, 7, 1), roll(shifted, -1, 1))
        zstar[q] = shifted

    for k, m in enumerate(codes):
        dx, dy = steps_of(m)
        tile = packed[k * 8:(k + 1) * 8, :]
        if dx and dy:
            edge = zstar[corner_dir[dx, dy], pl.ds(15 if dx == 1 else 0, 1), :]
            if dy == -1:
                edge = roll(jnp.broadcast_to(edge, (8, 128)), 120, 1)
            tile = jnp.where(lane[0:8] >= 120, edge, tile)
        outbox[k, 0:8, :] = tile
        if dy == 0:
            for i, q in enumerate(plus_x if dx == 1 else minus_x):
                outbox[k, 8 + i:9 + i, :] = zstar[q, pl.ds(15 if dx == 1 else 0, 1), :]
        elif dx == 0:
            face = jnp.zeros((16, 128), F32)
            for i, q in enumerate(plus_y if dy == 1 else minus_y):
                moved = roll(zstar[q], 8 * i + (8 if dy == 1 else 0), 1)
                face = jnp.where(lane // 8 == i, moved, face)
            outbox[k, 8:24, :] = face

    pl.semaphore_wait(barrier, len(peers))
    notes = []
    for k, m in enumerate(codes):
        copy = pltpu.make_async_remote_copy(
            src_ref=outbox.at[k, pl.ds(0, rows_of(m))],
            dst_ref=inbox.at[k, pl.ds(0, rows_of(m))],
            send_sem=note_send.at[k], recv_sem=note_recv.at[k],
            device_id=device(*steps_of(m)), device_id_type=MESH)
        copy.start()
        notes.append(copy)

    kept = own * jnp.where(code == 4, 1.0, 0.0)
    tab[...] = jnp.zeros_like(tab)
    tab[0:26, 0:256] = kept
    cells, dirs, slots = links_ref[0], links_ref[1], links_ref[2]

    def step_along(axis):
        value = jnp.zeros((2, 512), F32)
        for q in range(1, 19):
            if vel[q][axis]:
                value = jnp.where(dirs == q, float(vel[q][axis]), value)
        return value

    step_x, step_y, step_z = step_along(0), step_along(1), step_along(2)
    half = lax.broadcasted_iota(jnp.int32, (2, 512), 1) // 256
    bx = lax.broadcasted_iota(jnp.int32, (2, 512), 0)
    cell_x, cell_y, cell_z = cells // 64, cells // 8 % 8, cells % 8
    mid_x = ((gx * 2 + bx) * 8 + cell_x).astype(F32) + 0.5 * step_x
    mid_y = ((gy * 2 + half) * 8 + cell_y).astype(F32) + 0.5 * step_y
    mid_z = cell_z.astype(F32) + 0.5 * step_z
    scale = jnp.where(dirs < 7, 6.0 / 18.0, 6.0 / 36.0)
    place = half * 64 + cells % 64
    fdirs = dirs.astype(F32)

    features = jnp.concatenate(list(split3(tab[0:16, 0:256])), axis=0)
    resting, arriving, targets = [], [], []
    for b in range(2):
        slot = slots[b:b + 1, :]
        chosen = jnp.where(
            lax.broadcasted_iota(jnp.int32, (256, 512), 0) == slot, 1.0, 0.0).astype(BF16)
        resting.append(jnp.dot(features, chosen, preferred_element_type=F32))
        arriving.append(jnp.where(
            lax.broadcasted_iota(jnp.int32, (128, 512), 0) + 256 == slot,
            1.0, 0.0).astype(BF16))
        targets.append(jnp.where(
            lax.broadcasted_iota(jnp.int32, (128, 512), 0) == place[b:b + 1, :],
            1.0, 0.0).astype(BF16))

    for q in range(19):
        sx, sy, _ = vel[q]
        if sx or sy:
            zstar[q] = roll(roll(zstar[q], 8 * sy, 1), sx, 0)

    for copy in notes:
        copy.wait_recv()

    incoming = inbox[:, 0:8, :].reshape(64, 128)
    incoming = jnp.concatenate([incoming, jnp.zeros((64, 128), F32)], axis=0).T
    tab[0:26, 256:384] = incoming[0:26, :]
    table_ref[:, 0, :] = tab[0:26, 0:320]
    features = jnp.concatenate(list(split3(tab[0:16, 256:384])), axis=0)
    dense = []
    for b in range(2):
        def at(value):
            return value[b:b + 1, :]

        g = resting[b] + jnp.dot(features, arriving[b], preferred_element_type=F32)
        g = g[0:16] + g[16:32] + g[32:48]
        rel_x, rel_y, rel_z = at(mid_x) - g[0:1], at(mid_y) - g[1:2], at(mid_z) - g[2:3]
        wall_x = g[3:4] + g[7:8] * rel_z - g[8:9] * rel_y
        wall_y = g[4:5] + g[8:9] * rel_x - g[6:7] * rel_z
        wall_z = g[5:6] + g[6:7] * rel_y - g[7:8] * rel_x
        correction = at(scale) * (
            at(step_x) * wall_x + at(step_y) * wall_y + at(step_z) * wall_z)
        in_row = lax.broadcasted_iota(jnp.int32, (8, 512), 0) == at(cell_x)
        values = [p.astype(F32) for p in split3(correction)] + [at(fdirs)]
        spread = jnp.concatenate(
            [jnp.where(in_row, value, 0.0) for value in values], axis=0).astype(BF16)
        dense.append(lax.dot_general(spread, targets[b], (((1,), (1,)), ((), ())),
                                     preferred_element_type=F32))
    correction = jnp.concatenate([d[0:8] + d[8:16] + d[16:24] for d in dense], axis=0)
    link_dir = jnp.concatenate([d[24:32] for d in dense], axis=0)

    region_of = {steps_of(m): k for k, m in enumerate(codes)}
    for q in range(19):
        sx, sy, _ = vel[q]
        value = zstar[q]
        edge_lane = lane < 8 if sy == 1 else lane >= 120
        if sy:
            i = (plus_y if sy == 1 else minus_y).index(q)
            ghost = inbox[region_of[0, sy], 8:24, :]
            ghost = roll(ghost, -8 * i + (0 if sy == 1 else 120), 1)
            value = jnp.where(edge_lane, roll(ghost, sx, 0), value)
        if sx:
            i = (plus_x if sx == 1 else minus_x).index(q)
            line = inbox[region_of[sx, 0], 8 + i:9 + i, :]
            if sy:
                line = roll(jnp.broadcast_to(line, (8, 128)), 8 * sy, 1)
                corner = inbox[region_of[sx, sy], 0:8, :]
                corner = roll(corner, 8, 1) if sy == 1 else corner
                line = jnp.where(edge_lane[0:8], corner, line)[0:1]
            value = jnp.where(row == (0 if sx == 1 else 15), line, value)
        if q:
            value = jnp.where(link_dir == float(opp[q]), star[opp[q]] - correction, value)
        final[q * 16:(q + 1) * 16, :] = value

    wide = lax.broadcasted_iota(jnp.int32, (24, 128), 1) < 64
    holds = [jnp.broadcast_to(owner_ref[n // 2:n // 2 + 1, n % 2:n % 2 + 1], (24, 128))
             for n in range(4)]
    pieces = []
    for k in range(4):
        for b in range(2):
            first = final[pl.ds(b * 8 + 2 * k, 24, stride=16), :]
            second = final[pl.ds(b * 8 + 2 * k + 1, 24, stride=16), :]
            pieces.append(jnp.where(wide, first, roll(second, 64, 1)))
            pieces.append(jnp.where(wide, roll(first, 64, 1), second))
    sends = []
    for d in list(range(1, nx)) + [0]:
        to = lax.rem(gx + d, nx)
        here = [hold == to for hold in holds]
        for k in range(4):
            value = jnp.zeros((24, 128), F32)
            for n in range(4):
                value = jnp.where(here[n], pieces[4 * k + n], value)
            parcel[d, :, 0, k * 128:(k + 1) * 128] = value[0:19]
        if d:
            copy = pltpu.make_async_remote_copy(
                src_ref=parcel.at[d], dst_ref=blocks_ref.at[gx],
                send_sem=block_send.at[d - 1], recv_sem=block_recv.at[d - 1],
                device_id=(to, gy), device_id_type=MESH)
        else:
            copy = pltpu.make_async_copy(parcel.at[0], blocks_ref.at[gx], local_sem)
        copy.start()
        sends.append(copy)
    for copy in notes:
        copy.wait_send()
    for copy in sends:
        copy.wait()


def body(pdf, grains, grain_moves, owner_map, link_lists):
    nx, ny = lax.axis_size("gx"), lax.axis_size("gy")
    vmem = pl.BlockSpec(memory_space=pltpu.VMEM)
    blocks, table = pl.pallas_call(
        functools.partial(kernel, nx, ny),
        out_shape=(jax.ShapeDtypeStruct((nx, 19, 1, 512), F32),
                   jax.ShapeDtypeStruct((26, 1, 320), F32)),
        in_specs=[pl.BlockSpec(memory_space=pltpu.HBM)] * 5,
        out_specs=(pl.BlockSpec(memory_space=pl.ANY), vmem),
        scratch_shapes=[
            pltpu.VMEM(pdf.shape, F32),
            pltpu.VMEM(grains.shape, F32),
            pltpu.VMEM(grain_moves.shape, jnp.int32),
            pltpu.VMEM(owner_map.shape, jnp.int32),
            pltpu.VMEM(link_lists.shape, jnp.int32),
            pltpu.SemaphoreType.DMA((5,)),
            pltpu.VMEM((19, 16, 128), F32),
            pltpu.VMEM((19, 16, 128), F32),
            pltpu.VMEM((384, 128), F32),
            pltpu.VMEM((32, 256), F32),
            pltpu.VMEM((32, 384), F32),
            pltpu.VMEM((8, 24, 128), F32),
            pltpu.VMEM((8, 24, 128), F32),
            pltpu.VMEM((nx, 19, 1, 512), F32),
            pltpu.SemaphoreType.DMA((8,)),
            pltpu.SemaphoreType.DMA((8,)),
            pltpu.SemaphoreType.DMA((nx - 1,)),
            pltpu.SemaphoreType.DMA((nx - 1,)),
            pltpu.SemaphoreType.DMA,
        ],
        compiler_params=pltpu.CompilerParams(
            collective_id=0, has_side_effects=True, vmem_limit_bytes=64 * 1024 * 1024 - 128 * 1024),
        name="slab_step",
    )(pdf, grains, grain_moves, owner_map, link_lists)
    return blocks.transpose(0, 2, 1, 3), table


def solution(mesh):
    in_specs = (
        P(None, "gx", "gy"),
        P(None, "gx", "gy"),
        P("gx", "gy"),
        P("gx", "gy"),
        P(None, "gx", "gy"),
    )
    out_specs = (P("gx", "gy", None, None), P(None, "gx", "gy"))
    return jax.shard_map(body, mesh=mesh, in_specs=in_specs, out_specs=out_specs, check_vma=False)
```

```python
import functools

import jax
import jax.numpy as jnp
import numpy as np
from jax import lax
from jax.experimental import pallas as pl
from jax.experimental.pallas import tpu as pltpu
from jax.sharding import PartitionSpec as P

MESH = pl.DeviceIdType.MESH
F32 = jnp.float32
BF16 = jnp.bfloat16

vel = [
    (0, 0, 0), (1, 0, 0), (-1, 0, 0), (0, 1, 0), (0, -1, 0), (0, 0, 1), (0, 0, -1),
    (1, 1, 0), (-1, -1, 0), (1, -1, 0), (-1, 1, 0),
    (1, 0, 1), (-1, 0, -1), (1, 0, -1), (-1, 0, 1),
    (0, 1, 1), (0, -1, -1), (0, 1, -1), (0, -1, 1),
]
opp = [0, 2, 1, 4, 3, 6, 5, 8, 7, 10, 9, 12, 11, 14, 13, 16, 15, 18, 17]
wts = [1.0 / 3.0] + [1.0 / 18.0] * 6 + [1.0 / 36.0] * 12
codes = (0, 1, 2, 3, 5, 6, 7, 8)
plus_x = [q for q in range(19) if vel[q][0] == 1]
minus_x = [q for q in range(19) if vel[q][0] == -1]
plus_y = [q for q in range(19) if vel[q][1] == 1]
minus_y = [q for q in range(19) if vel[q][1] == -1]
corner_dir = {(1, 1): 7, (-1, -1): 8, (1, -1): 9, (-1, 1): 10}


def steps_of(code):
    return code // 3 - 1, code % 3 - 1


def rows_of(code):
    dx, dy = steps_of(code)
    return 24 if dx == 0 else 16 if dy == 0 else 8


def roll(value, shift, axis):
    size = value.shape[axis]
    shift = shift % size
    return value if shift == 0 else pltpu.roll(value, shift, axis)


def split3(value):
    high = value.astype(BF16)
    rest = value - high.astype(F32)
    mid = rest.astype(BF16)
    low = (rest - mid.astype(F32)).astype(BF16)
    return high, mid, low


def collide(load):
    f = [load(q) for q in range(19)]
    sx = [f[q] for q in plus_x]
    density = functools.reduce(lambda a, b: a + b, f)

    def total(qs):
        return functools.reduce(lambda a, b: a + b, [f[q] for q in qs])

    px, mx = total(plus_x), total(minus_x)
    py, my = total(plus_y), total(minus_y)
    plus_z = [q for q in range(19) if vel[q][2] == 1]
    minus_z = [q for q in range(19) if vel[q][2] == -1]
    pz, mz = total(plus_z), total(minus_z)
    inverse = 1.0 / density
    ux, uy, uz = (px - mx) * inverse, (py - my) * inverse, (pz - mz) * inverse
    third = density * (1.0 / 3.0)
    dux, duy, duz = density * ux, density * uy, density * uz
    xx = (px + mx) - third - dux * ux
    yy = (py + my) - third - duy * uy
    zz = (pz + mz) - third - duz * uz
    xy = (f[7] + f[8]) - (f[9] + f[10]) - dux * uy
    xz = (f[11] + f[12]) - (f[13] + f[14]) - dux * uz
    yz = (f[15] + f[16]) - (f[17] + f[18]) - duy * uz
    contracted = xx * xx + yy * yy + zz * zz + 2.0 * (xy * xy + xz * xz + yz * yz)
    shear = (1.5 / 0.8) * inverse * jnp.sqrt(2.0 * contracted)
    scaled = 20.0 * shear
    viscosity = 0.01 + (0.1 - 0.01) * lax.rsqrt(jnp.sqrt(1.0 + scaled * scaled))
    omega = 1.0 / (3.0 * viscosity + 0.5)
    base = 1.0 - 1.5 * (ux * ux + uy * uy + uz * uz)
    keep = 1.0 - omega
    gain = {w: omega * density * w for w in set(wts)}
    out = []
    for q in range(19):
        c = None
        for step, u in zip(vel[q], (ux, uy, uz)):
            if step:
                term = u if step > 0 else -u
                c = term if c is None else c + term
        bracket = base if c is None else base + c * (3.0 + 4.5 * c)
        out.append(keep * f[q] + gain[wts[q]] * bracket)
    return out


def kernel(nx, ny, pdf_hbm, grains_hbm, moves_hbm, owner_hbm, links_hbm,
           blocks_ref, table_ref,
           pdf_ref, grains_ref, moves_ref, owner_ref, links_ref, load_sem, star, zstar, final, pad, tab, outbox, inbox, parcel,
           note_send, note_recv, block_send, block_recv, local_sem):
    gx = lax.axis_index("gx")
    gy = lax.axis_index("gy")

    def device(dx, dy):
        return (lax.rem(gx + dx + nx, nx), lax.rem(gy + dy + ny, ny))

    loads = [
        pltpu.make_async_copy(source, held, load_sem.at[i])
        for i, (source, held) in enumerate((
            (grains_hbm, grains_ref), (moves_hbm, moves_ref), (pdf_hbm, pdf_ref),
            (owner_hbm, owner_ref), (links_hbm, links_ref)))
    ]
    for load in loads:
        load.start()
    barrier = pltpu.get_barrier_semaphore()
    peers = [steps_of(m) for m in codes] + [(d, 0) for d in range(2, nx - 1)]
    for dx, dy in peers:
        pl.semaphore_signal(barrier, inc=1, device_id=device(dx, dy), device_id_type=MESH)

    lane = lax.broadcasted_iota(jnp.int32, (16, 128), 1)
    row = lax.broadcasted_iota(jnp.int32, (16, 128), 0)
    depth = lane % 8

    pad[...] = jnp.zeros_like(pad)
    for load in loads[:2]:
        load.wait()
    own = grains_ref[:, 0, :]
    pad[0:26, :] = own
    code = moves_ref[...]
    kind = lax.broadcasted_iota(jnp.int32, (16, 256), 0)
    match = jnp.where(kind == code, 1.0, 0.0)
    before = jnp.where(
        lax.broadcasted_iota(jnp.int32, (256, 256), 0)
        < lax.broadcasted_iota(jnp.int32, (256, 256), 1), 1.0, 0.0)
    counts = jnp.dot(match.astype(BF16), before.astype(BF16), preferred_element_type=F32)
    rank = jnp.sum(match * counts, axis=0, keepdims=True).astype(jnp.int32)
    region = jnp.where(code > 4, code - 1, code)
    target = jnp.where(code == 4, -1, region * 8 + rank)
    slot = lax.broadcasted_iota(jnp.int32, (64, 256), 0)
    placing = jnp.where(slot == target, 1.0, 0.0).astype(BF16)
    parts = jnp.concatenate(list(split3(pad[...])) + [jnp.zeros((32, 256), BF16)], axis=0)
    packed = lax.dot_general(placing, parts, (((1,), (1,)), ((), ())),
                             preferred_element_type=F32)
    packed = packed + roll(packed, -32, 1) + roll(packed, -64, 1)
    packed = jnp.where(lax.broadcasted_iota(jnp.int32, (64, 128), 1) < 32, packed, 0.0)

    loads[2].wait()
    collided = collide(lambda q: pdf_ref[q])
    for q in range(19):
        star[q] = collided[q]
        shifted = collided[q]
        if vel[q][2] == 1:
            shifted = jnp.where(depth == 0, roll(shifted, -7, 1), roll(shifted, 1, 1))
        elif vel[q][2] == -1:
            shifted = jnp.where(depth == 7, roll(shifted, 7, 1), roll(shifted, -1, 1))
        zstar[q] = shifted

    for k, m in enumerate(codes):
        dx, dy = steps_of(m)
        tile = packed[k * 8:(k + 1) * 8, :]
        if dx and dy:
            edge = zstar[corner_dir[dx, dy], pl.ds(15 if dx == 1 else 0, 1), :]
            if dy == -1:
                edge = roll(jnp.broadcast_to(edge, (8, 128)), 120, 1)
            tile = jnp.where(lane[0:8] >= 120, edge, tile)
        outbox[k, 0:8, :] = tile
        if dy == 0:
            for i, q in enumerate(plus_x if dx == 1 else minus_x):
                outbox[k, 8 + i:9 + i, :] = zstar[q, pl.ds(15 if dx == 1 else 0, 1), :]
        elif dx == 0:
            face = jnp.zeros((16, 128), F32)
            for i, q in enumerate(plus_y if dy == 1 else minus_y):
                moved = roll(zstar[q], 8 * i + (8 if dy == 1 else 0), 1)
                face = jnp.where(lane // 8 == i, moved, face)
            outbox[k, 8:24, :] = face

    pl.semaphore_wait(barrier, len(peers))
    notes = []
    for k, m in enumerate(codes):
        copy = pltpu.make_async_remote_copy(
            src_ref=outbox.at[k, pl.ds(0, rows_of(m))],
            dst_ref=inbox.at[k, pl.ds(0, rows_of(m))],
            send_sem=note_send.at[k], recv_sem=note_recv.at[k],
            device_id=device(*steps_of(m)), device_id_type=MESH)
        copy.start()
        notes.append(copy)

    kept = own * jnp.where(code == 4, 1.0, 0.0)
    tab[...] = jnp.zeros_like(tab)
    tab[0:26, 0:256] = kept
    for load in loads[3:]:
        load.wait()
    cells, dirs, slots = links_ref[0], links_ref[1], links_ref[2]

    def step_along(axis):
        value = jnp.zeros((2, 512), F32)
        for q in range(1, 19):
            if vel[q][axis]:
                value = jnp.where(dirs == q, float(vel[q][axis]), value)
        return value

    step_x, step_y, step_z = step_along(0), step_along(1), step_along(2)
    half = lax.broadcasted_iota(jnp.int32, (2, 512), 1) // 256
    bx = lax.broadcasted_iota(jnp.int32, (2, 512), 0)
    cell_x, cell_y, cell_z = cells // 64, cells // 8 % 8, cells % 8
    mid_x = ((gx * 2 + bx) * 8 + cell_x).astype(F32) + 0.5 * step_x
    mid_y = ((gy * 2 + half) * 8 + cell_y).astype(F32) + 0.5 * step_y
    mid_z = cell_z.astype(F32) + 0.5 * step_z
    scale = jnp.where(dirs < 7, 6.0 / 18.0, 6.0 / 36.0)
    place = half * 64 + cells % 64
    fdirs = dirs.astype(F32)

    features = jnp.concatenate(list(split3(tab[0:16, 0:256])), axis=0)
    resting, arriving, targets = [], [], []
    for b in range(2):
        slot = slots[b:b + 1, :]
        chosen = jnp.where(
            lax.broadcasted_iota(jnp.int32, (256, 512), 0) == slot, 1.0, 0.0).astype(BF16)
        resting.append(jnp.dot(features, chosen, preferred_element_type=F32))
        arriving.append(jnp.where(
            lax.broadcasted_iota(jnp.int32, (128, 512), 0) + 256 == slot,
            1.0, 0.0).astype(BF16))
        targets.append(jnp.where(
            lax.broadcasted_iota(jnp.int32, (128, 512), 0) == place[b:b + 1, :],
            1.0, 0.0).astype(BF16))

    for q in range(19):
        sx, sy, _ = vel[q]
        if sx or sy:
            zstar[q] = roll(roll(zstar[q], 8 * sy, 1), sx, 0)

    for copy in notes:
        copy.wait_recv()

    incoming = inbox[:, 0:8, :].reshape(64, 128)
    incoming = jnp.concatenate([incoming, jnp.zeros((64, 128), F32)], axis=0).T
    tab[0:26, 256:384] = incoming[0:26, :]
    table_ref[:, 0, :] = tab[0:26, 0:320]
    features = jnp.concatenate(list(split3(tab[0:16, 256:384])), axis=0)
    dense = []
    for b in range(2):
        def at(value):
            return value[b:b + 1, :]

        g = resting[b] + jnp.dot(features, arriving[b], preferred_element_type=F32)
        g = g[0:16] + g[16:32] + g[32:48]
        rel_x, rel_y, rel_z = at(mid_x) - g[0:1], at(mid_y) - g[1:2], at(mid_z) - g[2:3]
        wall_x = g[3:4] + g[7:8] * rel_z - g[8:9] * rel_y
        wall_y = g[4:5] + g[8:9] * rel_x - g[6:7] * rel_z
        wall_z = g[5:6] + g[6:7] * rel_y - g[7:8] * rel_x
        correction = at(scale) * (
            at(step_x) * wall_x + at(step_y) * wall_y + at(step_z) * wall_z)
        in_row = lax.broadcasted_iota(jnp.int32, (8, 512), 0) == at(cell_x)
        values = [p.astype(F32) for p in split3(correction)] + [at(fdirs)]
        spread = jnp.concatenate(
            [jnp.where(in_row, value, 0.0) for value in values], axis=0).astype(BF16)
        dense.append(lax.dot_general(spread, targets[b], (((1,), (1,)), ((), ())),
                                     preferred_element_type=F32))
    correction = jnp.concatenate([d[0:8] + d[8:16] + d[16:24] for d in dense], axis=0)
    link_dir = jnp.concatenate([d[24:32] for d in dense], axis=0)

    region_of = {steps_of(m): k for k, m in enumerate(codes)}
    for q in range(19):
        sx, sy, _ = vel[q]
        value = zstar[q]
        edge_lane = lane < 8 if sy == 1 else lane >= 120
        if sy:
            i = (plus_y if sy == 1 else minus_y).index(q)
            ghost = inbox[region_of[0, sy], 8:24, :]
            ghost = roll(ghost, -8 * i + (0 if sy == 1 else 120), 1)
            value = jnp.where(edge_lane, roll(ghost, sx, 0), value)
        if sx:
            i = (plus_x if sx == 1 else minus_x).index(q)
            line = inbox[region_of[sx, 0], 8 + i:9 + i, :]
            if sy:
                line = roll(jnp.broadcast_to(line, (8, 128)), 8 * sy, 1)
                corner = inbox[region_of[sx, sy], 0:8, :]
                corner = roll(corner, 8, 1) if sy == 1 else corner
                line = jnp.where(edge_lane[0:8], corner, line)[0:1]
            value = jnp.where(row == (0 if sx == 1 else 15), line, value)
        if q:
            value = jnp.where(link_dir == float(opp[q]), star[opp[q]] - correction, value)
        final[q * 16:(q + 1) * 16, :] = value

    wide = lax.broadcasted_iota(jnp.int32, (24, 128), 1) < 64
    holds = [jnp.broadcast_to(owner_ref[n // 2:n // 2 + 1, n % 2:n % 2 + 1], (24, 128))
             for n in range(4)]
    pieces = []
    for k in range(4):
        for b in range(2):
            first = final[pl.ds(b * 8 + 2 * k, 24, stride=16), :]
            second = final[pl.ds(b * 8 + 2 * k + 1, 24, stride=16), :]
            pieces.append(jnp.where(wide, first, roll(second, 64, 1)))
            pieces.append(jnp.where(wide, roll(first, 64, 1), second))
    sends = []
    order = sorted(range(1, nx), key=lambda d: abs(2 * d - nx))
    for d in order + [0]:
        to = lax.rem(gx + d, nx)
        here = [hold == to for hold in holds]
        for k in range(4):
            value = jnp.zeros((24, 128), F32)
            for n in range(4):
                value = jnp.where(here[n], pieces[4 * k + n], value)
            parcel[d, :, 0, k * 128:(k + 1) * 128] = value[0:19]
        if d:
            copy = pltpu.make_async_remote_copy(
                src_ref=parcel.at[d], dst_ref=blocks_ref.at[gx],
                send_sem=block_send.at[d - 1], recv_sem=block_recv.at[d - 1],
                device_id=(to, gy), device_id_type=MESH)
        else:
            copy = pltpu.make_async_copy(parcel.at[0], blocks_ref.at[gx], local_sem)
        copy.start()
        sends.append(copy)
    for copy in notes:
        copy.wait_send()
    for copy in sends:
        copy.wait()


def hand_over(blocks_in, table_in, blocks_out, table_out, sem):
    copies = [pltpu.make_async_copy(blocks_in, blocks_out, sem.at[0]),
              pltpu.make_async_copy(table_in, table_out, sem.at[1])]
    for copy in copies:
        copy.start()
    for copy in copies:
        copy.wait()


def body(pdf, grains, grain_moves, owner_map, link_lists):
    nx, ny = lax.axis_size("gx"), lax.axis_size("gy")
    vmem = pl.BlockSpec(memory_space=pltpu.VMEM)
    blocks, table = pl.pallas_call(
        functools.partial(kernel, nx, ny),
        out_shape=(jax.ShapeDtypeStruct((nx, 19, 1, 512), F32),
                   jax.ShapeDtypeStruct((26, 1, 320), F32)),
        in_specs=[pl.BlockSpec(memory_space=pltpu.HBM)] * 5,
        out_specs=(pl.BlockSpec(memory_space=pl.ANY), vmem),
        scratch_shapes=[
            pltpu.VMEM(pdf.shape, F32),
            pltpu.VMEM(grains.shape, F32),
            pltpu.VMEM(grain_moves.shape, jnp.int32),
            pltpu.VMEM(owner_map.shape, jnp.int32),
            pltpu.VMEM(link_lists.shape, jnp.int32),
            pltpu.SemaphoreType.DMA((5,)),
            pltpu.VMEM((19, 16, 128), F32),
            pltpu.VMEM((19, 16, 128), F32),
            pltpu.VMEM((384, 128), F32),
            pltpu.VMEM((32, 256), F32),
            pltpu.VMEM((32, 384), F32),
            pltpu.VMEM((8, 24, 128), F32),
            pltpu.VMEM((8, 24, 128), F32),
            pltpu.VMEM((nx, 19, 1, 512), F32),
            pltpu.SemaphoreType.DMA((8,)),
            pltpu.SemaphoreType.DMA((8,)),
            pltpu.SemaphoreType.DMA((nx - 1,)),
            pltpu.SemaphoreType.DMA((nx - 1,)),
            pltpu.SemaphoreType.DMA,
        ],
        compiler_params=pltpu.CompilerParams(
            collective_id=0, has_side_effects=True, vmem_limit_bytes=64 * 1024 * 1024),
        name="slab_step",
    )(pdf, grains, grain_moves, owner_map, link_lists)
    hbm = pl.BlockSpec(memory_space=pltpu.HBM)
    blocks, table = pl.pallas_call(
        hand_over,
        out_shape=(jax.ShapeDtypeStruct(blocks.shape, F32),
                   jax.ShapeDtypeStruct(table.shape, F32)),
        in_specs=[hbm, hbm], out_specs=(hbm, hbm),
        scratch_shapes=[pltpu.SemaphoreType.DMA((2,))],
        compiler_params=pltpu.CompilerParams(vmem_limit_bytes=64 * 1024 * 1024),
        name="hand_over",
    )(blocks, table)
    return blocks.transpose(0, 2, 1, 3), table


def solution(mesh):
    in_specs = (
        P(None, "gx", "gy"),
        P(None, "gx", "gy"),
        P("gx", "gy"),
        P("gx", "gy"),
        P(None, "gx", "gy"),
    )
    out_specs = (P("gx", "gy", None, None), P(None, "gx", "gy"))
    return jax.shard_map(body, mesh=mesh, in_specs=in_specs, out_specs=out_specs, check_vma=False)
```

```python
import functools

import jax
import jax.numpy as jnp
import numpy as np
from jax import lax
from jax.experimental import pallas as pl
from jax.experimental.pallas import tpu as pltpu
from jax.sharding import PartitionSpec as P

MESH = pl.DeviceIdType.MESH
F32 = jnp.float32
BF16 = jnp.bfloat16

vel = [
    (0, 0, 0), (1, 0, 0), (-1, 0, 0), (0, 1, 0), (0, -1, 0), (0, 0, 1), (0, 0, -1),
    (1, 1, 0), (-1, -1, 0), (1, -1, 0), (-1, 1, 0),
    (1, 0, 1), (-1, 0, -1), (1, 0, -1), (-1, 0, 1),
    (0, 1, 1), (0, -1, -1), (0, 1, -1), (0, -1, 1),
]
opp = [0, 2, 1, 4, 3, 6, 5, 8, 7, 10, 9, 12, 11, 14, 13, 16, 15, 18, 17]
wts = [1.0 / 3.0] + [1.0 / 18.0] * 6 + [1.0 / 36.0] * 12
codes = (0, 1, 2, 3, 5, 6, 7, 8)
plus_x = [q for q in range(19) if vel[q][0] == 1]
minus_x = [q for q in range(19) if vel[q][0] == -1]
plus_y = [q for q in range(19) if vel[q][1] == 1]
minus_y = [q for q in range(19) if vel[q][1] == -1]
corner_dir = {(1, 1): 7, (-1, -1): 8, (1, -1): 9, (-1, 1): 10}


def steps_of(code):
    return code // 3 - 1, code % 3 - 1


def rows_of(code):
    dx, dy = steps_of(code)
    return 24 if dx == 0 else 16 if dy == 0 else 8


def roll(value, shift, axis):
    size = value.shape[axis]
    shift = shift % size
    return value if shift == 0 else pltpu.roll(value, shift, axis)


def split3(value):
    high = value.astype(BF16)
    rest = value - high.astype(F32)
    mid = rest.astype(BF16)
    low = (rest - mid.astype(F32)).astype(BF16)
    return high, mid, low


def collide(load):
    f = [load(q) for q in range(19)]
    sx = [f[q] for q in plus_x]
    density = functools.reduce(lambda a, b: a + b, f)

    def total(qs):
        return functools.reduce(lambda a, b: a + b, [f[q] for q in qs])

    px, mx = total(plus_x), total(minus_x)
    py, my = total(plus_y), total(minus_y)
    plus_z = [q for q in range(19) if vel[q][2] == 1]
    minus_z = [q for q in range(19) if vel[q][2] == -1]
    pz, mz = total(plus_z), total(minus_z)
    inverse = 1.0 / density
    ux, uy, uz = (px - mx) * inverse, (py - my) * inverse, (pz - mz) * inverse
    third = density * (1.0 / 3.0)
    dux, duy, duz = density * ux, density * uy, density * uz
    xx = (px + mx) - third - dux * ux
    yy = (py + my) - third - duy * uy
    zz = (pz + mz) - third - duz * uz
    xy = (f[7] + f[8]) - (f[9] + f[10]) - dux * uy
    xz = (f[11] + f[12]) - (f[13] + f[14]) - dux * uz
    yz = (f[15] + f[16]) - (f[17] + f[18]) - duy * uz
    contracted = xx * xx + yy * yy + zz * zz + 2.0 * (xy * xy + xz * xz + yz * yz)
    shear = (1.5 / 0.8) * inverse * jnp.sqrt(2.0 * contracted)
    scaled = 20.0 * shear
    viscosity = 0.01 + (0.1 - 0.01) * lax.rsqrt(jnp.sqrt(1.0 + scaled * scaled))
    omega = 1.0 / (3.0 * viscosity + 0.5)
    base = 1.0 - 1.5 * (ux * ux + uy * uy + uz * uz)
    keep = 1.0 - omega
    gain = {w: omega * density * w for w in set(wts)}
    out = []
    for q in range(19):
        c = None
        for step, u in zip(vel[q], (ux, uy, uz)):
            if step:
                term = u if step > 0 else -u
                c = term if c is None else c + term
        bracket = base if c is None else base + c * (3.0 + 4.5 * c)
        out.append(keep * f[q] + gain[wts[q]] * bracket)
    return out


def kernel(nx, ny, pdf_hbm, grains_hbm, moves_hbm, owner_hbm, links_hbm,
           blocks_ref, table_ref,
           pdf_ref, grains_ref, moves_ref, owner_ref, links_ref, load_sem, star, zstar, final, pad, tab, outbox, inbox, parcel,
           note_send, note_recv, block_send, block_recv, local_sem):
    gx = lax.axis_index("gx")
    gy = lax.axis_index("gy")

    def device(dx, dy):
        return (lax.rem(gx + dx + nx, nx), lax.rem(gy + dy + ny, ny))

    loads = [
        pltpu.make_async_copy(source, held, load_sem.at[i])
        for i, (source, held) in enumerate((
            (grains_hbm, grains_ref), (moves_hbm, moves_ref), (pdf_hbm, pdf_ref),
            (owner_hbm, owner_ref), (links_hbm, links_ref)))
    ]
    for load in loads:
        load.start()
    barrier = pltpu.get_barrier_semaphore()
    peers = [steps_of(m) for m in codes] + [(d, 0) for d in range(2, nx - 1)]
    for dx, dy in peers:
        pl.semaphore_signal(barrier, inc=1, device_id=device(dx, dy), device_id_type=MESH)

    lane = lax.broadcasted_iota(jnp.int32, (16, 128), 1)
    row = lax.broadcasted_iota(jnp.int32, (16, 128), 0)
    depth = lane % 8

    pad[...] = jnp.zeros_like(pad)
    for load in loads[:2]:
        load.wait()
    own = grains_ref[:, 0, :]
    pad[0:26, :] = own
    code = moves_ref[...]
    kind = lax.broadcasted_iota(jnp.int32, (16, 256), 0)
    match = jnp.where(kind == code, 1.0, 0.0)
    before = jnp.where(
        lax.broadcasted_iota(jnp.int32, (256, 256), 0)
        < lax.broadcasted_iota(jnp.int32, (256, 256), 1), 1.0, 0.0)
    counts = jnp.dot(match.astype(BF16), before.astype(BF16), preferred_element_type=F32)
    rank = jnp.sum(match * counts, axis=0, keepdims=True).astype(jnp.int32)
    region = jnp.where(code > 4, code - 1, code)
    target = jnp.where(code == 4, -1, region * 8 + rank)
    slot = lax.broadcasted_iota(jnp.int32, (64, 256), 0)
    placing = jnp.where(slot == target, 1.0, 0.0).astype(BF16)
    parts = jnp.concatenate(list(split3(pad[...])) + [jnp.zeros((32, 256), BF16)], axis=0)
    packed = lax.dot_general(placing, parts, (((1,), (1,)), ((), ())),
                             preferred_element_type=F32)
    packed = packed + roll(packed, -32, 1) + roll(packed, -64, 1)
    packed = jnp.where(lax.broadcasted_iota(jnp.int32, (64, 128), 1) < 32, packed, 0.0)

    loads[2].wait()
    collided = collide(lambda q: pdf_ref[q])
    for q in range(19):
        star[q] = collided[q]
        shifted = collided[q]
        if vel[q][2] == 1:
            shifted = jnp.where(depth == 0, roll(shifted, -7, 1), roll(shifted, 1, 1))
        elif vel[q][2] == -1:
            shifted = jnp.where(depth == 7, roll(shifted, 7, 1), roll(shifted, -1, 1))
        zstar[q] = shifted

    for k, m in enumerate(codes):
        dx, dy = steps_of(m)
        tile = packed[k * 8:(k + 1) * 8, :]
        if dx and dy:
            edge = zstar[corner_dir[dx, dy], pl.ds(15 if dx == 1 else 0, 1), :]
            if dy == -1:
                edge = roll(jnp.broadcast_to(edge, (8, 128)), 120, 1)
            tile = jnp.where(lane[0:8] >= 120, edge, tile)
        outbox[k, 0:8, :] = tile
        if dy == 0:
            for i, q in enumerate(plus_x if dx == 1 else minus_x):
                outbox[k, 8 + i:9 + i, :] = zstar[q, pl.ds(15 if dx == 1 else 0, 1), :]
        elif dx == 0:
            face = jnp.zeros((16, 128), F32)
            for i, q in enumerate(plus_y if dy == 1 else minus_y):
                moved = roll(zstar[q], 8 * i + (8 if dy == 1 else 0), 1)
                face = jnp.where(lane // 8 == i, moved, face)
            outbox[k, 8:24, :] = face

    pl.semaphore_wait(barrier, len(peers))
    notes = []
    for k, m in enumerate(codes):
        copy = pltpu.make_async_remote_copy(
            src_ref=outbox.at[k, pl.ds(0, rows_of(m))],
            dst_ref=inbox.at[k, pl.ds(0, rows_of(m))],
            send_sem=note_send.at[k], recv_sem=note_recv.at[k],
            device_id=device(*steps_of(m)), device_id_type=MESH)
        copy.start()
        notes.append(copy)

    kept = own * jnp.where(code == 4, 1.0, 0.0)
    tab[...] = jnp.zeros_like(tab)
    tab[0:26, 0:256] = kept
    for load in loads[3:]:
        load.wait()
    cells, dirs, slots = links_ref[0], links_ref[1], links_ref[2]

    def step_along(axis):
        value = jnp.zeros((2, 512), F32)
        for q in range(1, 19):
            if vel[q][axis]:
                value = jnp.where(dirs == q, float(vel[q][axis]), value)
        return value

    step_x, step_y, step_z = step_along(0), step_along(1), step_along(2)
    half = lax.broadcasted_iota(jnp.int32, (2, 512), 1) // 256
    bx = lax.broadcasted_iota(jnp.int32, (2, 512), 0)
    cell_x, cell_y, cell_z = cells // 64, cells // 8 % 8, cells % 8
    mid_x = ((gx * 2 + bx) * 8 + cell_x).astype(F32) + 0.5 * step_x
    mid_y = ((gy * 2 + half) * 8 + cell_y).astype(F32) + 0.5 * step_y
    mid_z = cell_z.astype(F32) + 0.5 * step_z
    scale = jnp.where(dirs < 7, 6.0 / 18.0, 6.0 / 36.0)
    place = half * 64 + cells % 64
    fdirs = dirs.astype(F32)

    features = jnp.concatenate(list(split3(tab[0:16, 0:256])), axis=0)
    resting, arriving, targets = [], [], []
    for b in range(2):
        slot = slots[b:b + 1, :]
        chosen = jnp.where(
            lax.broadcasted_iota(jnp.int32, (256, 512), 0) == slot, 1.0, 0.0).astype(BF16)
        resting.append(jnp.dot(features, chosen, preferred_element_type=F32))
        arriving.append(jnp.where(
            lax.broadcasted_iota(jnp.int32, (128, 512), 0) + 256 == slot,
            1.0, 0.0).astype(BF16))
        targets.append(jnp.where(
            lax.broadcasted_iota(jnp.int32, (128, 512), 0) == place[b:b + 1, :],
            1.0, 0.0).astype(BF16))

    for q in range(19):
        sx, sy, _ = vel[q]
        if sx or sy:
            zstar[q] = roll(roll(zstar[q], 8 * sy, 1), sx, 0)

    for copy in notes:
        copy.wait_recv()

    incoming = inbox[:, 0:8, :].reshape(64, 128)
    incoming = jnp.concatenate([incoming, jnp.zeros((64, 128), F32)], axis=0).T
    tab[0:26, 256:384] = incoming[0:26, :]
    table_ref[:, 0, :] = tab[0:26, 0:320]
    features = jnp.concatenate(list(split3(tab[0:16, 256:384])), axis=0)
    dense = []
    for b in range(2):
        def at(value):
            return value[b:b + 1, :]

        g = resting[b] + jnp.dot(features, arriving[b], preferred_element_type=F32)
        g = g[0:16] + g[16:32] + g[32:48]
        rel_x, rel_y, rel_z = at(mid_x) - g[0:1], at(mid_y) - g[1:2], at(mid_z) - g[2:3]
        wall_x = g[3:4] + g[7:8] * rel_z - g[8:9] * rel_y
        wall_y = g[4:5] + g[8:9] * rel_x - g[6:7] * rel_z
        wall_z = g[5:6] + g[6:7] * rel_y - g[7:8] * rel_x
        correction = at(scale) * (
            at(step_x) * wall_x + at(step_y) * wall_y + at(step_z) * wall_z)
        in_row = lax.broadcasted_iota(jnp.int32, (8, 512), 0) == at(cell_x)
        values = [p.astype(F32) for p in split3(correction)] + [at(fdirs)]
        spread = jnp.concatenate(
            [jnp.where(in_row, value, 0.0) for value in values], axis=0).astype(BF16)
        dense.append(lax.dot_general(spread, targets[b], (((1,), (1,)), ((), ())),
                                     preferred_element_type=F32))
    correction = jnp.concatenate([d[0:8] + d[8:16] + d[16:24] for d in dense], axis=0)
    link_dir = jnp.concatenate([d[24:32] for d in dense], axis=0)

    region_of = {steps_of(m): k for k, m in enumerate(codes)}
    for q in range(19):
        sx, sy, _ = vel[q]
        value = zstar[q]
        edge_lane = lane < 8 if sy == 1 else lane >= 120
        if sy:
            i = (plus_y if sy == 1 else minus_y).index(q)
            ghost = inbox[region_of[0, sy], 8:24, :]
            ghost = roll(ghost, -8 * i + (0 if sy == 1 else 120), 1)
            value = jnp.where(edge_lane, roll(ghost, sx, 0), value)
        if sx:
            i = (plus_x if sx == 1 else minus_x).index(q)
            line = inbox[region_of[sx, 0], 8 + i:9 + i, :]
            if sy:
                line = roll(jnp.broadcast_to(line, (8, 128)), 8 * sy, 1)
                corner = inbox[region_of[sx, sy], 0:8, :]
                corner = roll(corner, 8, 1) if sy == 1 else corner
                line = jnp.where(edge_lane[0:8], corner, line)[0:1]
            value = jnp.where(row == (0 if sx == 1 else 15), line, value)
        if q:
            value = jnp.where(link_dir == float(opp[q]), star[opp[q]] - correction, value)
        final[q * 16:(q + 1) * 16, :] = value

    wide = lax.broadcasted_iota(jnp.int32, (24, 128), 1) < 64
    holds = [jnp.broadcast_to(owner_ref[n // 2:n // 2 + 1, n % 2:n % 2 + 1], (24, 128))
             for n in range(4)]
    pieces = []
    for k in range(4):
        for b in range(2):
            first = final[pl.ds(b * 8 + 2 * k, 24, stride=16), :]
            second = final[pl.ds(b * 8 + 2 * k + 1, 24, stride=16), :]
            pieces.append(jnp.where(wide, first, roll(second, 64, 1)))
            pieces.append(jnp.where(wide, roll(first, 64, 1), second))
    sends = []
    order = sorted(range(1, nx), key=lambda d: abs(2 * d - nx))
    for d in order + [0]:
        to = lax.rem(gx + d, nx)
        here = [hold == to for hold in holds]
        for k in range(4):
            value = jnp.zeros((24, 128), F32)
            for n in range(4):
                value = jnp.where(here[n], pieces[4 * k + n], value)
            parcel[d, :, 0, k * 128:(k + 1) * 128] = value[0:19]
        if d:
            copy = pltpu.make_async_remote_copy(
                src_ref=parcel.at[d], dst_ref=blocks_ref.at[gx],
                send_sem=block_send.at[d - 1], recv_sem=block_recv.at[d - 1],
                device_id=(to, gy), device_id_type=MESH)
        else:
            copy = pltpu.make_async_copy(parcel.at[0], blocks_ref.at[gx], local_sem)
        copy.start()
        sends.append(copy)
    for copy in notes:
        copy.wait_send()
    for copy in sends:
        copy.wait()


def hand_over(blocks_in, table_in, blocks_out, table_out, blocks_here, table_here,
              load_sem, store_sem):
    count = blocks_in.shape[0]
    pairs = [(blocks_in.at[i], blocks_here.at[i], blocks_out.at[i]) for i in range(count)]
    pairs.append((table_in, table_here, table_out))
    loads = [pltpu.make_async_copy(a, b, load_sem.at[i]) for i, (a, b, _) in enumerate(pairs)]
    stores = [pltpu.make_async_copy(b, c, store_sem.at[i]) for i, (_, b, c) in enumerate(pairs)]
    for load in loads:
        load.start()
    for load, store in zip(loads, stores):
        load.wait()
        store.start()
    for store in stores:
        store.wait()


def body(pdf, grains, grain_moves, owner_map, link_lists):
    nx, ny = lax.axis_size("gx"), lax.axis_size("gy")
    vmem = pl.BlockSpec(memory_space=pltpu.VMEM)
    blocks, table = pl.pallas_call(
        functools.partial(kernel, nx, ny),
        out_shape=(jax.ShapeDtypeStruct((nx, 19, 1, 512), F32),
                   jax.ShapeDtypeStruct((26, 1, 320), F32)),
        in_specs=[pl.BlockSpec(memory_space=pltpu.HBM)] * 5,
        out_specs=(pl.BlockSpec(memory_space=pl.ANY), vmem),
        scratch_shapes=[
            pltpu.VMEM(pdf.shape, F32),
            pltpu.VMEM(grains.shape, F32),
            pltpu.VMEM(grain_moves.shape, jnp.int32),
            pltpu.VMEM(owner_map.shape, jnp.int32),
            pltpu.VMEM(link_lists.shape, jnp.int32),
            pltpu.SemaphoreType.DMA((5,)),
            pltpu.VMEM((19, 16, 128), F32),
            pltpu.VMEM((19, 16, 128), F32),
            pltpu.VMEM((384, 128), F32),
            pltpu.VMEM((32, 256), F32),
            pltpu.VMEM((32, 384), F32),
            pltpu.VMEM((8, 24, 128), F32),
            pltpu.VMEM((8, 24, 128), F32),
            pltpu.VMEM((nx, 19, 1, 512), F32),
            pltpu.SemaphoreType.DMA((8,)),
            pltpu.SemaphoreType.DMA((8,)),
            pltpu.SemaphoreType.DMA((nx - 1,)),
            pltpu.SemaphoreType.DMA((nx - 1,)),
            pltpu.SemaphoreType.DMA,
        ],
        compiler_params=pltpu.CompilerParams(
            collective_id=0, has_side_effects=True, vmem_limit_bytes=64 * 1024 * 1024),
        name="slab_step",
    )(pdf, grains, grain_moves, owner_map, link_lists)
    hbm = pl.BlockSpec(memory_space=pltpu.HBM)
    blocks, table = pl.pallas_call(
        hand_over,
        out_shape=(jax.ShapeDtypeStruct(blocks.shape, F32),
                   jax.ShapeDtypeStruct(table.shape, F32)),
        in_specs=[hbm, hbm], out_specs=(hbm, hbm),
        scratch_shapes=[
            pltpu.VMEM(blocks.shape, F32),
            pltpu.VMEM(table.shape, F32),
            pltpu.SemaphoreType.DMA((nx + 1,)),
            pltpu.SemaphoreType.DMA((nx + 1,)),
        ],
        compiler_params=pltpu.CompilerParams(vmem_limit_bytes=64 * 1024 * 1024),
        name="hand_over",
    )(blocks, table)
    return blocks.transpose(0, 2, 1, 3), table


def solution(mesh):
    in_specs = (
        P(None, "gx", "gy"),
        P(None, "gx", "gy"),
        P("gx", "gy"),
        P("gx", "gy"),
        P(None, "gx", "gy"),
    )
    out_specs = (P("gx", "gy", None, None), P(None, "gx", "gy"))
    return jax.shard_map(body, mesh=mesh, in_specs=in_specs, out_specs=out_specs, check_vma=False)
```

```python
import functools

import jax
import jax.numpy as jnp
import numpy as np
from jax import lax
from jax.experimental import pallas as pl
from jax.experimental.pallas import tpu as pltpu
from jax.sharding import PartitionSpec as P

MESH = pl.DeviceIdType.MESH
F32 = jnp.float32
BF16 = jnp.bfloat16

vel = [
    (0, 0, 0), (1, 0, 0), (-1, 0, 0), (0, 1, 0), (0, -1, 0), (0, 0, 1), (0, 0, -1),
    (1, 1, 0), (-1, -1, 0), (1, -1, 0), (-1, 1, 0),
    (1, 0, 1), (-1, 0, -1), (1, 0, -1), (-1, 0, 1),
    (0, 1, 1), (0, -1, -1), (0, 1, -1), (0, -1, 1),
]
opp = [0, 2, 1, 4, 3, 6, 5, 8, 7, 10, 9, 12, 11, 14, 13, 16, 15, 18, 17]
wts = [1.0 / 3.0] + [1.0 / 18.0] * 6 + [1.0 / 36.0] * 12
codes = (0, 1, 2, 3, 5, 6, 7, 8)
plus_x = [q for q in range(19) if vel[q][0] == 1]
minus_x = [q for q in range(19) if vel[q][0] == -1]
plus_y = [q for q in range(19) if vel[q][1] == 1]
minus_y = [q for q in range(19) if vel[q][1] == -1]
corner_dir = {(1, 1): 7, (-1, -1): 8, (1, -1): 9, (-1, 1): 10}


def steps_of(code):
    return code // 3 - 1, code % 3 - 1


def rows_of(code):
    dx, dy = steps_of(code)
    return 24 if dx == 0 else 16 if dy == 0 else 8


def roll(value, shift, axis):
    size = value.shape[axis]
    shift = shift % size
    return value if shift == 0 else pltpu.roll(value, shift, axis)


def split3(value):
    high = value.astype(BF16)
    rest = value - high.astype(F32)
    mid = rest.astype(BF16)
    low = (rest - mid.astype(F32)).astype(BF16)
    return high, mid, low


def collide(load):
    f = [load(q) for q in range(19)]
    sx = [f[q] for q in plus_x]
    density = functools.reduce(lambda a, b: a + b, f)

    def total(qs):
        return functools.reduce(lambda a, b: a + b, [f[q] for q in qs])

    px, mx = total(plus_x), total(minus_x)
    py, my = total(plus_y), total(minus_y)
    plus_z = [q for q in range(19) if vel[q][2] == 1]
    minus_z = [q for q in range(19) if vel[q][2] == -1]
    pz, mz = total(plus_z), total(minus_z)
    inverse = 1.0 / density
    ux, uy, uz = (px - mx) * inverse, (py - my) * inverse, (pz - mz) * inverse
    third = density * (1.0 / 3.0)
    dux, duy, duz = density * ux, density * uy, density * uz
    xx = (px + mx) - third - dux * ux
    yy = (py + my) - third - duy * uy
    zz = (pz + mz) - third - duz * uz
    xy = (f[7] + f[8]) - (f[9] + f[10]) - dux * uy
    xz = (f[11] + f[12]) - (f[13] + f[14]) - dux * uz
    yz = (f[15] + f[16]) - (f[17] + f[18]) - duy * uz
    contracted = xx * xx + yy * yy + zz * zz + 2.0 * (xy * xy + xz * xz + yz * yz)
    shear = (1.5 / 0.8) * inverse * jnp.sqrt(2.0 * contracted)
    scaled = 20.0 * shear
    viscosity = 0.01 + (0.1 - 0.01) * lax.rsqrt(jnp.sqrt(1.0 + scaled * scaled))
    omega = 1.0 / (3.0 * viscosity + 0.5)
    base = 1.0 - 1.5 * (ux * ux + uy * uy + uz * uz)
    keep = 1.0 - omega
    gain = {w: omega * density * w for w in set(wts)}
    out = []
    for q in range(19):
        c = None
        for step, u in zip(vel[q], (ux, uy, uz)):
            if step:
                term = u if step > 0 else -u
                c = term if c is None else c + term
        bracket = base if c is None else base + c * (3.0 + 4.5 * c)
        out.append(keep * f[q] + gain[wts[q]] * bracket)
    return out


def kernel(nx, ny, pdf_hbm, grains_hbm, moves_hbm, owner_hbm, links_hbm,
           bulk_ref, fix_ref, table_ref,
           pdf_ref, grains_ref, moves_ref, owner_ref, links_ref, load_sem, star, zstar, pad, tab, outbox, inbox, parcel, patch,
           note_send, note_recv, block_send, block_recv, patch_send, patch_recv, local_sem):
    gx = lax.axis_index("gx")
    gy = lax.axis_index("gy")

    def device(dx, dy):
        return (lax.rem(gx + dx + nx, nx), lax.rem(gy + dy + ny, ny))

    loads = [
        pltpu.make_async_copy(source, held, load_sem.at[i])
        for i, (source, held) in enumerate((
            (grains_hbm, grains_ref), (moves_hbm, moves_ref), (pdf_hbm, pdf_ref),
            (owner_hbm, owner_ref), (links_hbm, links_ref)))
    ]
    for load in loads:
        load.start()
    barrier = pltpu.get_barrier_semaphore()
    peers = [steps_of(m) for m in codes] + [(d, 0) for d in range(2, nx - 1)]
    for dx, dy in peers:
        pl.semaphore_signal(barrier, inc=1, device_id=device(dx, dy), device_id_type=MESH)

    lane = lax.broadcasted_iota(jnp.int32, (16, 128), 1)
    row = lax.broadcasted_iota(jnp.int32, (16, 128), 0)
    depth = lane % 8

    pad[...] = jnp.zeros_like(pad)
    for load in loads[:2]:
        load.wait()
    own = grains_ref[:, 0, :]
    pad[0:26, :] = own
    code = moves_ref[...]
    kind = lax.broadcasted_iota(jnp.int32, (16, 256), 0)
    match = jnp.where(kind == code, 1.0, 0.0)
    before = jnp.where(
        lax.broadcasted_iota(jnp.int32, (256, 256), 0)
        < lax.broadcasted_iota(jnp.int32, (256, 256), 1), 1.0, 0.0)
    counts = jnp.dot(match.astype(BF16), before.astype(BF16), preferred_element_type=F32)
    rank = jnp.sum(match * counts, axis=0, keepdims=True).astype(jnp.int32)
    region = jnp.where(code > 4, code - 1, code)
    target = jnp.where(code == 4, -1, region * 8 + rank)
    slot = lax.broadcasted_iota(jnp.int32, (64, 256), 0)
    placing = jnp.where(slot == target, 1.0, 0.0).astype(BF16)
    parts = jnp.concatenate(list(split3(pad[...])) + [jnp.zeros((32, 256), BF16)], axis=0)
    packed = lax.dot_general(placing, parts, (((1,), (1,)), ((), ())),
                             preferred_element_type=F32)
    packed = packed + roll(packed, -32, 1) + roll(packed, -64, 1)
    packed = jnp.where(lax.broadcasted_iota(jnp.int32, (64, 128), 1) < 32, packed, 0.0)

    loads[2].wait()
    collided = collide(lambda q: pdf_ref[q])
    for q in range(19):
        star[q] = collided[q]
        shifted = collided[q]
        if vel[q][2] == 1:
            shifted = jnp.where(depth == 0, roll(shifted, -7, 1), roll(shifted, 1, 1))
        elif vel[q][2] == -1:
            shifted = jnp.where(depth == 7, roll(shifted, 7, 1), roll(shifted, -1, 1))
        zstar[q] = shifted

    for k, m in enumerate(codes):
        dx, dy = steps_of(m)
        tile = packed[k * 8:(k + 1) * 8, :]
        if dx and dy:
            edge = zstar[corner_dir[dx, dy], pl.ds(15 if dx == 1 else 0, 1), :]
            if dy == -1:
                edge = roll(jnp.broadcast_to(edge, (8, 128)), 120, 1)
            tile = jnp.where(lane[0:8] >= 120, edge, tile)
        outbox[k, 0:8, :] = tile
        if dy == 0:
            for i, q in enumerate(plus_x if dx == 1 else minus_x):
                outbox[k, 8 + i:9 + i, :] = zstar[q, pl.ds(15 if dx == 1 else 0, 1), :]
        elif dx == 0:
            face = jnp.zeros((16, 128), F32)
            for i, q in enumerate(plus_y if dy == 1 else minus_y):
                moved = roll(zstar[q], 8 * i + (8 if dy == 1 else 0), 1)
                face = jnp.where(lane // 8 == i, moved, face)
            outbox[k, 8:24, :] = face

    pl.semaphore_wait(barrier, len(peers))
    notes = []
    for k, m in enumerate(codes):
        copy = pltpu.make_async_remote_copy(
            src_ref=outbox.at[k, pl.ds(0, rows_of(m))],
            dst_ref=inbox.at[k, pl.ds(0, rows_of(m))],
            send_sem=note_send.at[k], recv_sem=note_recv.at[k],
            device_id=device(*steps_of(m)), device_id_type=MESH)
        copy.start()
        notes.append(copy)

    for q in range(19):
        sx, sy, _ = vel[q]
        if sx or sy:
            zstar[q] = roll(roll(zstar[q], 8 * sy, 1), sx, 0)
    loads[3].wait()
    holds = [jnp.broadcast_to(owner_ref[n // 2:n // 2 + 1, n % 2:n % 2 + 1], (8, 128))
             for n in range(4)]
    wide = lane < 64
    sends = []

    def by_block(low, high):
        left = jnp.where(wide, low, roll(high, 64, 1))
        right = jnp.where(wide, roll(low, 64, 1), high)
        return [left[0:8], right[0:8], left[8:16], right[8:16]]

    def to_owners(tiles, box, out_ref, send_sems, recv_sems, local):
        for d in list(range(1, nx)) + [0]:
            to = lax.rem(gx + d, nx)
            mine = [hold == to for hold in holds]
            for p, tile in enumerate(tiles):
                value = jnp.zeros((8, 128), F32)
                for n in range(4):
                    value = jnp.where(mine[n], tile[n], value)
                box[d, p] = value
            if d:
                copy = pltpu.make_async_remote_copy(
                    src_ref=box.at[d], dst_ref=out_ref.at[gx],
                    send_sem=send_sems.at[d - 1], recv_sem=recv_sems.at[d - 1],
                    device_id=(to, gy), device_id_type=MESH)
            else:
                copy = pltpu.make_async_copy(box.at[0], out_ref.at[gx], local)
            copy.start()
            sends.append(copy)

    empty = jnp.zeros((16, 128), F32)
    to_owners([by_block(zstar[p], zstar[10 + p] if p < 9 else empty) for p in range(10)],
              parcel, bulk_ref, block_send, block_recv, local_sem.at[0])

    kept = own * jnp.where(code == 4, 1.0, 0.0)
    tab[...] = jnp.zeros_like(tab)
    tab[0:26, 0:256] = kept
    loads[4].wait()
    cells, dirs, slots = links_ref[0], links_ref[1], links_ref[2]

    def step_along(axis):
        value = jnp.zeros((2, 512), F32)
        for q in range(1, 19):
            if vel[q][axis]:
                value = jnp.where(dirs == q, float(vel[q][axis]), value)
        return value

    step_x, step_y, step_z = step_along(0), step_along(1), step_along(2)
    half = lax.broadcasted_iota(jnp.int32, (2, 512), 1) // 256
    bx = lax.broadcasted_iota(jnp.int32, (2, 512), 0)
    cell_x, cell_y, cell_z = cells // 64, cells // 8 % 8, cells % 8
    mid_x = ((gx * 2 + bx) * 8 + cell_x).astype(F32) + 0.5 * step_x
    mid_y = ((gy * 2 + half) * 8 + cell_y).astype(F32) + 0.5 * step_y
    mid_z = cell_z.astype(F32) + 0.5 * step_z
    scale = jnp.where(dirs < 7, 6.0 / 18.0, 6.0 / 36.0)
    place = half * 64 + cells % 64
    fdirs = dirs.astype(F32)

    features = jnp.concatenate(list(split3(tab[0:16, 0:256])), axis=0)
    resting, arriving, targets = [], [], []
    for b in range(2):
        slot = slots[b:b + 1, :]
        chosen = jnp.where(
            lax.broadcasted_iota(jnp.int32, (256, 512), 0) == slot, 1.0, 0.0).astype(BF16)
        resting.append(jnp.dot(features, chosen, preferred_element_type=F32))
        arriving.append(jnp.where(
            lax.broadcasted_iota(jnp.int32, (128, 512), 0) + 256 == slot,
            1.0, 0.0).astype(BF16))
        targets.append(jnp.where(
            lax.broadcasted_iota(jnp.int32, (128, 512), 0) == place[b:b + 1, :],
            1.0, 0.0).astype(BF16))

    for copy in notes:
        copy.wait_recv()

    incoming = inbox[:, 0:8, :].reshape(64, 128)
    incoming = jnp.concatenate([incoming, jnp.zeros((64, 128), F32)], axis=0).T
    tab[0:26, 256:384] = incoming[0:26, :]
    table_ref[:, 0, :] = tab[0:26, 0:320]
    features = jnp.concatenate(list(split3(tab[0:16, 256:384])), axis=0)
    dense = []
    for b in range(2):
        def at(value):
            return value[b:b + 1, :]

        g = resting[b] + jnp.dot(features, arriving[b], preferred_element_type=F32)
        g = g[0:16] + g[16:32] + g[32:48]
        rel_x, rel_y, rel_z = at(mid_x) - g[0:1], at(mid_y) - g[1:2], at(mid_z) - g[2:3]
        wall_x = g[3:4] + g[7:8] * rel_z - g[8:9] * rel_y
        wall_y = g[4:5] + g[8:9] * rel_x - g[6:7] * rel_z
        wall_z = g[5:6] + g[6:7] * rel_y - g[7:8] * rel_x
        correction = at(scale) * (
            at(step_x) * wall_x + at(step_y) * wall_y + at(step_z) * wall_z)
        in_row = lax.broadcasted_iota(jnp.int32, (8, 512), 0) == at(cell_x)
        values = [p.astype(F32) for p in split3(correction)] + [at(fdirs)]
        spread = jnp.concatenate(
            [jnp.where(in_row, value, 0.0) for value in values], axis=0).astype(BF16)
        dense.append(lax.dot_general(spread, targets[b], (((1,), (1,)), ((), ())),
                                     preferred_element_type=F32))
    correction = jnp.concatenate([d[0:8] + d[8:16] + d[16:24] for d in dense], axis=0)
    link_dir = jnp.concatenate([d[24:32] for d in dense], axis=0)

    region_of = {steps_of(m): k for k, m in enumerate(codes)}
    value = empty
    for q in range(1, 19):
        value = jnp.where(link_dir == float(q), star[q], value)
    links = by_block(value - correction, link_dir)
    sides = {}
    for sy, qs in ((1, plus_y), (-1, minus_y)):
        face = inbox[region_of[0, sy], 8:24, :]
        side = face
        for i, q in enumerate(qs):
            if vel[q][0]:
                side = jnp.where(lane // 8 == i, roll(face, vel[q][0], 0), side)
        sides[sy] = roll(side, 64, 1)
    margins = []
    row8, lane8 = row[0:8], lane[0:8]
    for n in range(4):
        sx = 1 if n < 2 else -1
        lines = jnp.zeros((8, 128), F32)
        for i, q in enumerate(plus_x if sx == 1 else minus_x):
            sy = vel[q][1]
            line = jnp.broadcast_to(inbox[region_of[sx, 0], 8 + i:9 + i, :], (8, 128))
            if sy:
                corner = inbox[region_of[sx, sy], 0:1, :]
                corner = roll(jnp.broadcast_to(corner, (8, 128)), 8 if sy == 1 else 0, 1)
                line = jnp.where(lane8 < 8 if sy == 1 else lane8 >= 120, corner,
                                 roll(line, 8 * sy, 1))
            lines = jnp.where(row8 == i, line, lines)
        side = sides[1 if n % 2 == 0 else -1][8 * (n // 2):8 * (n // 2) + 8]
        margin = jnp.where(wide[0:8], roll(lines, 64, 1) if n % 2 else lines, side)
        margin = jnp.where(lane8 == 112, float(n // 2), margin)
        margins.append(jnp.where(lane8 == 113, float(n % 2), margin))
    to_owners([links, margins], patch, fix_ref, patch_send, patch_recv, local_sem.at[1])
    for copy in notes:
        copy.wait_send()
    for copy in sends:
        copy.wait()


def settle(bulk_ref, fix_ref, table_in, blocks_ref, table_ref):
    table_ref[...] = table_in[...]
    lane = lax.broadcasted_iota(jnp.int32, (8, 128), 1)
    row = lax.broadcasted_iota(jnp.int32, (8, 128), 0)
    wide = lane < 64
    for a in range(bulk_ref.shape[0]):
        links, margin = fix_ref[a, 0], fix_ref[a, 1]
        turned = roll(links, 64, 1)
        link_value = jnp.where(wide, links, turned)
        link_dir = jnp.where(wide, turned, links)
        at_x = jnp.broadcast_to(margin[0:1, 112:113], (8, 128))
        at_y = jnp.broadcast_to(margin[0:1, 113:114], (8, 128))
        for p in range(10):
            value = bulk_ref[a, p]
            for half, q in ((0, p), (1, 10 + p)):
                if q > 18:
                    continue
                sx, sy, _ = vel[q]
                if sy:
                    i = (plus_y if sy == 1 else minus_y).index(q)
                    first = 64 * half + (0 if sy == 1 else 56)
                    inside = (lane >= first) & (lane < first + 8)
                    inside = inside & (at_y == (0.0 if sy == 1 else 1.0))
                    value = jnp.where(inside, roll(margin, first - 64 - 8 * i, 1), value)
                if sx:
                    i = (plus_x if sx == 1 else minus_x).index(q)
                    line = jnp.broadcast_to(margin[i:i + 1, :], (8, 128))
                    line = roll(line, 64, 1) if half else line
                    inside = (row == (0 if sx == 1 else 7)) & (wide if half == 0 else lane >= 64)
                    inside = inside & (at_x == (0.0 if sx == 1 else 1.0))
                    value = jnp.where(inside, line, value)
            wanted = jnp.where(wide, float(opp[p]) if p else -1.0,
                               float(opp[10 + p]) if p < 9 else -1.0)
            value = jnp.where(link_dir == wanted, link_value, value)
            moved = roll(value, 64, 1)
            low = jnp.where(wide, value, roll(moved, -1, 0))
            high = jnp.where(wide, moved, roll(value, -1, 0))
            for q, pairs in ((p, low), (10 + p, high)):
                if q < 19:
                    for k in range(4):
                        blocks_ref[a, q, :, k * 128:(k + 1) * 128] = pairs[2 * k:2 * k + 1, :]


def body(pdf, grains, grain_moves, owner_map, link_lists):
    nx, ny = lax.axis_size("gx"), lax.axis_size("gy")
    vmem = pl.BlockSpec(memory_space=pltpu.VMEM)
    bulk, fix, table = pl.pallas_call(
        functools.partial(kernel, nx, ny),
        out_shape=(jax.ShapeDtypeStruct((nx, 10, 8, 128), F32),
                   jax.ShapeDtypeStruct((nx, 2, 8, 128), F32),
                   jax.ShapeDtypeStruct((26, 1, 320), F32)),
        in_specs=[pl.BlockSpec(memory_space=pltpu.HBM)] * 5,
        out_specs=(pl.BlockSpec(memory_space=pl.ANY), pl.BlockSpec(memory_space=pl.ANY), vmem),
        scratch_shapes=[
            pltpu.VMEM(pdf.shape, F32),
            pltpu.VMEM(grains.shape, F32),
            pltpu.VMEM(grain_moves.shape, jnp.int32),
            pltpu.VMEM(owner_map.shape, jnp.int32),
            pltpu.VMEM(link_lists.shape, jnp.int32),
            pltpu.SemaphoreType.DMA((5,)),
            pltpu.VMEM((19, 16, 128), F32),
            pltpu.VMEM((19, 16, 128), F32),
            pltpu.VMEM((32, 256), F32),
            pltpu.VMEM((32, 384), F32),
            pltpu.VMEM((8, 24, 128), F32),
            pltpu.VMEM((8, 24, 128), F32),
            pltpu.VMEM((nx, 10, 8, 128), F32),
            pltpu.VMEM((nx, 2, 8, 128), F32),
            pltpu.SemaphoreType.DMA((8,)),
            pltpu.SemaphoreType.DMA((8,)),
            pltpu.SemaphoreType.DMA((nx - 1,)),
            pltpu.SemaphoreType.DMA((nx - 1,)),
            pltpu.SemaphoreType.DMA((nx - 1,)),
            pltpu.SemaphoreType.DMA((nx - 1,)),
            pltpu.SemaphoreType.DMA((2,)),
        ],
        compiler_params=pltpu.CompilerParams(
            collective_id=0, has_side_effects=True, vmem_limit_bytes=64 * 1024 * 1024),
        name="slab_step",
    )(pdf, grains, grain_moves, owner_map, link_lists)
    blocks, table = pl.pallas_call(
        settle,
        out_shape=(jax.ShapeDtypeStruct((nx, 19, 1, 512), F32),
                   jax.ShapeDtypeStruct(table.shape, F32)),
        in_specs=[vmem] * 3, out_specs=(vmem, vmem),
        compiler_params=pltpu.CompilerParams(vmem_limit_bytes=64 * 1024 * 1024),
        name="settle",
    )(bulk, fix, table)
    return blocks.transpose(0, 2, 1, 3), table


def solution(mesh):
    in_specs = (
        P(None, "gx", "gy"),
        P(None, "gx", "gy"),
        P("gx", "gy"),
        P("gx", "gy"),
        P(None, "gx", "gy"),
    )
    out_specs = (P("gx", "gy", None, None), P(None, "gx", "gy"))
    return jax.shard_map(body, mesh=mesh, in_specs=in_specs, out_specs=out_specs, check_vma=False)
```

```python
import functools

import jax
import jax.numpy as jnp
import numpy as np
from jax import lax
from jax.experimental import pallas as pl
from jax.experimental.pallas import tpu as pltpu
from jax.sharding import PartitionSpec as P

MESH = pl.DeviceIdType.MESH
F32 = jnp.float32
BF16 = jnp.bfloat16

vel = [
    (0, 0, 0), (1, 0, 0), (-1, 0, 0), (0, 1, 0), (0, -1, 0), (0, 0, 1), (0, 0, -1),
    (1, 1, 0), (-1, -1, 0), (1, -1, 0), (-1, 1, 0),
    (1, 0, 1), (-1, 0, -1), (1, 0, -1), (-1, 0, 1),
    (0, 1, 1), (0, -1, -1), (0, 1, -1), (0, -1, 1),
]
opp = [0, 2, 1, 4, 3, 6, 5, 8, 7, 10, 9, 12, 11, 14, 13, 16, 15, 18, 17]
wts = [1.0 / 3.0] + [1.0 / 18.0] * 6 + [1.0 / 36.0] * 12
codes = (0, 1, 2, 3, 5, 6, 7, 8)
plus_x = [q for q in range(19) if vel[q][0] == 1]
minus_x = [q for q in range(19) if vel[q][0] == -1]
plus_y = [q for q in range(19) if vel[q][1] == 1]
minus_y = [q for q in range(19) if vel[q][1] == -1]
corner_dir = {(1, 1): 7, (-1, -1): 8, (1, -1): 9, (-1, 1): 10}


def steps_of(code):
    return code // 3 - 1, code % 3 - 1


def rows_of(code):
    dx, dy = steps_of(code)
    return 24 if dx == 0 else 16 if dy == 0 else 8


def roll(value, shift, axis):
    size = value.shape[axis]
    shift = shift % size
    return value if shift == 0 else pltpu.roll(value, shift, axis)


def split3(value):
    high = value.astype(BF16)
    rest = value - high.astype(F32)
    mid = rest.astype(BF16)
    low = (rest - mid.astype(F32)).astype(BF16)
    return high, mid, low


def collide(load):
    f = [load(q) for q in range(19)]
    sx = [f[q] for q in plus_x]
    density = functools.reduce(lambda a, b: a + b, f)

    def total(qs):
        return functools.reduce(lambda a, b: a + b, [f[q] for q in qs])

    px, mx = total(plus_x), total(minus_x)
    py, my = total(plus_y), total(minus_y)
    plus_z = [q for q in range(19) if vel[q][2] == 1]
    minus_z = [q for q in range(19) if vel[q][2] == -1]
    pz, mz = total(plus_z), total(minus_z)
    inverse = 1.0 / density
    ux, uy, uz = (px - mx) * inverse, (py - my) * inverse, (pz - mz) * inverse
    third = density * (1.0 / 3.0)
    dux, duy, duz = density * ux, density * uy, density * uz
    xx = (px + mx) - third - dux * ux
    yy = (py + my) - third - duy * uy
    zz = (pz + mz) - third - duz * uz
    xy = (f[7] + f[8]) - (f[9] + f[10]) - dux * uy
    xz = (f[11] + f[12]) - (f[13] + f[14]) - dux * uz
    yz = (f[15] + f[16]) - (f[17] + f[18]) - duy * uz
    contracted = xx * xx + yy * yy + zz * zz + 2.0 * (xy * xy + xz * xz + yz * yz)
    shear = (1.5 / 0.8) * inverse * jnp.sqrt(2.0 * contracted)
    scaled = 20.0 * shear
    viscosity = 0.01 + (0.1 - 0.01) * lax.rsqrt(jnp.sqrt(1.0 + scaled * scaled))
    omega = 1.0 / (3.0 * viscosity + 0.5)
    base = 1.0 - 1.5 * (ux * ux + uy * uy + uz * uz)
    keep = 1.0 - omega
    gain = {w: omega * density * w for w in set(wts)}
    out = []
    for q in range(19):
        c = None
        for step, u in zip(vel[q], (ux, uy, uz)):
            if step:
                term = u if step > 0 else -u
                c = term if c is None else c + term
        bracket = base if c is None else base + c * (3.0 + 4.5 * c)
        out.append(keep * f[q] + gain[wts[q]] * bracket)
    return out


def kernel(nx, ny, pdf_hbm, grains_hbm, moves_hbm, owner_hbm, links_hbm,
           bulk_ref, fix_ref, table_ref,
           pdf_ref, grains_ref, moves_ref, owner_ref, links_ref, load_sem, star, zstar, pad, tab, outbox, inbox, parcel, patch,
           note_send, note_recv, block_send, block_recv, patch_send, patch_recv, local_sem):
    gx = lax.axis_index("gx")
    gy = lax.axis_index("gy")

    def device(dx, dy):
        return (lax.rem(gx + dx + nx, nx), lax.rem(gy + dy + ny, ny))

    loads = [
        pltpu.make_async_copy(source, held, load_sem.at[i])
        for i, (source, held) in enumerate((
            (grains_hbm, grains_ref), (moves_hbm, moves_ref), (pdf_hbm, pdf_ref),
            (owner_hbm, owner_ref), (links_hbm, links_ref)))
    ]
    for load in loads:
        load.start()
    barrier = pltpu.get_barrier_semaphore()
    peers = [steps_of(m) for m in codes] + [(d, 0) for d in range(2, nx - 1)]
    for dx, dy in peers:
        pl.semaphore_signal(barrier, inc=1, device_id=device(dx, dy), device_id_type=MESH)

    lane = lax.broadcasted_iota(jnp.int32, (16, 128), 1)
    row = lax.broadcasted_iota(jnp.int32, (16, 128), 0)
    depth = lane % 8

    pad[...] = jnp.zeros_like(pad)
    for load in loads[:2]:
        load.wait()
    own = grains_ref[:, 0, :]
    pad[0:26, :] = own
    code = moves_ref[...]
    kind = lax.broadcasted_iota(jnp.int32, (16, 256), 0)
    match = jnp.where(kind == code, 1.0, 0.0)
    before = jnp.where(
        lax.broadcasted_iota(jnp.int32, (256, 256), 0)
        < lax.broadcasted_iota(jnp.int32, (256, 256), 1), 1.0, 0.0)
    counts = jnp.dot(match.astype(BF16), before.astype(BF16), preferred_element_type=F32)
    rank = jnp.sum(match * counts, axis=0, keepdims=True).astype(jnp.int32)
    region = jnp.where(code > 4, code - 1, code)
    target = jnp.where(code == 4, -1, region * 8 + rank)
    slot = lax.broadcasted_iota(jnp.int32, (64, 256), 0)
    placing = jnp.where(slot == target, 1.0, 0.0).astype(BF16)
    parts = jnp.concatenate(list(split3(pad[...])) + [jnp.zeros((32, 256), BF16)], axis=0)
    packed = lax.dot_general(placing, parts, (((1,), (1,)), ((), ())),
                             preferred_element_type=F32)
    packed = packed + roll(packed, -32, 1) + roll(packed, -64, 1)
    packed = jnp.where(lax.broadcasted_iota(jnp.int32, (64, 128), 1) < 32, packed, 0.0)

    loads[2].wait()
    collided = collide(lambda q: pdf_ref[q])
    for q in range(19):
        star[q] = collided[q]
        shifted = collided[q]
        if vel[q][2] == 1:
            shifted = jnp.where(depth == 0, roll(shifted, -7, 1), roll(shifted, 1, 1))
        elif vel[q][2] == -1:
            shifted = jnp.where(depth == 7, roll(shifted, 7, 1), roll(shifted, -1, 1))
        zstar[q] = shifted

    for k, m in enumerate(codes):
        dx, dy = steps_of(m)
        tile = packed[k * 8:(k + 1) * 8, :]
        if dx and dy:
            edge = zstar[corner_dir[dx, dy], pl.ds(15 if dx == 1 else 0, 1), :]
            if dy == -1:
                edge = roll(jnp.broadcast_to(edge, (8, 128)), 120, 1)
            tile = jnp.where(lane[0:8] >= 120, edge, tile)
        outbox[k, 0:8, :] = tile
        if dy == 0:
            for i, q in enumerate(plus_x if dx == 1 else minus_x):
                outbox[k, 8 + i:9 + i, :] = zstar[q, pl.ds(15 if dx == 1 else 0, 1), :]
        elif dx == 0:
            face = jnp.zeros((16, 128), F32)
            for i, q in enumerate(plus_y if dy == 1 else minus_y):
                moved = roll(zstar[q], 8 * i + (8 if dy == 1 else 0), 1)
                face = jnp.where(lane // 8 == i, moved, face)
            outbox[k, 8:24, :] = face

    pl.semaphore_wait(barrier, len(peers))
    notes = []
    for k, m in enumerate(codes):
        copy = pltpu.make_async_remote_copy(
            src_ref=outbox.at[k, pl.ds(0, rows_of(m))],
            dst_ref=inbox.at[k, pl.ds(0, rows_of(m))],
            send_sem=note_send.at[k], recv_sem=note_recv.at[k],
            device_id=device(*steps_of(m)), device_id_type=MESH)
        copy.start()
        notes.append(copy)

    for q in range(19):
        sx, sy, _ = vel[q]
        if sx or sy:
            zstar[q] = roll(roll(zstar[q], 8 * sy, 1), sx, 0)
    loads[3].wait()
    holds = [jnp.broadcast_to(owner_ref[n // 2:n // 2 + 1, n % 2:n % 2 + 1], (8, 128))
             for n in range(4)]
    wide = lane < 64
    sends = []

    def by_block(low, high):
        left = jnp.where(wide, low, roll(high, 64, 1))
        right = jnp.where(wide, roll(low, 64, 1), high)
        return [left[0:8], right[0:8], left[8:16], right[8:16]]

    def to_owners(tiles, box, out_ref, send_sems, recv_sems, local):
        for d in list(range(1, nx)) + [0]:
            to = lax.rem(gx + d, nx)
            mine = [hold == to for hold in holds]
            for p, tile in enumerate(tiles):
                value = jnp.zeros((8, 128), F32)
                for n in range(4):
                    value = jnp.where(mine[n], tile[n], value)
                box[d, p] = value
            if d:
                copy = pltpu.make_async_remote_copy(
                    src_ref=box.at[d], dst_ref=out_ref.at[gx],
                    send_sem=send_sems.at[d - 1], recv_sem=recv_sems.at[d - 1],
                    device_id=(to, gy), device_id_type=MESH)
            else:
                copy = pltpu.make_async_copy(box.at[0], out_ref.at[gx], local)
            copy.start()
            sends.append(copy)

    empty = jnp.zeros((16, 128), F32)
    to_owners([by_block(zstar[p], zstar[10 + p] if p < 9 else empty) for p in range(10)],
              parcel, bulk_ref, block_send, block_recv, local_sem.at[0])

    kept = own * jnp.where(code == 4, 1.0, 0.0)
    tab[...] = jnp.zeros_like(tab)
    tab[0:26, 0:256] = kept
    loads[4].wait()
    cells, dirs, slots = links_ref[0], links_ref[1], links_ref[2]

    def step_along(axis):
        value = jnp.zeros((2, 512), F32)
        for q in range(1, 19):
            if vel[q][axis]:
                value = jnp.where(dirs == q, float(vel[q][axis]), value)
        return value

    step_x, step_y, step_z = step_along(0), step_along(1), step_along(2)
    half = lax.broadcasted_iota(jnp.int32, (2, 512), 1) // 256
    bx = lax.broadcasted_iota(jnp.int32, (2, 512), 0)
    cell_x, cell_y, cell_z = cells // 64, cells // 8 % 8, cells % 8
    mid_x = ((gx * 2 + bx) * 8 + cell_x).astype(F32) + 0.5 * step_x
    mid_y = ((gy * 2 + half) * 8 + cell_y).astype(F32) + 0.5 * step_y
    mid_z = cell_z.astype(F32) + 0.5 * step_z
    scale = jnp.where(dirs < 7, 6.0 / 18.0, 6.0 / 36.0)
    place = half * 64 + cells % 64
    fdirs = dirs.astype(F32)

    features = jnp.concatenate(list(split3(tab[0:16, 0:256])), axis=0)
    resting, arriving, targets = [], [], []
    for b in range(2):
        slot = slots[b:b + 1, :]
        chosen = jnp.where(
            lax.broadcasted_iota(jnp.int32, (256, 512), 0) == slot, 1.0, 0.0).astype(BF16)
        resting.append(jnp.dot(features, chosen, preferred_element_type=F32))
        arriving.append(jnp.where(
            lax.broadcasted_iota(jnp.int32, (128, 512), 0) + 256 == slot,
            1.0, 0.0).astype(BF16))
        targets.append(jnp.where(
            lax.broadcasted_iota(jnp.int32, (128, 512), 0) == place[b:b + 1, :],
            1.0, 0.0).astype(BF16))

    for copy in notes:
        copy.wait_recv()

    incoming = inbox[:, 0:8, :].reshape(64, 128)
    incoming = jnp.concatenate([incoming, jnp.zeros((64, 128), F32)], axis=0).T
    tab[0:26, 256:384] = incoming[0:26, :]
    table_ref[:, 0, :] = tab[0:26, 0:320]
    features = jnp.concatenate(list(split3(tab[0:16, 256:384])), axis=0)
    dense = []
    for b in range(2):
        def at(value):
            return value[b:b + 1, :]

        g = resting[b] + jnp.dot(features, arriving[b], preferred_element_type=F32)
        g = g[0:16] + g[16:32] + g[32:48]
        rel_x, rel_y, rel_z = at(mid_x) - g[0:1], at(mid_y) - g[1:2], at(mid_z) - g[2:3]
        wall_x = g[3:4] + g[7:8] * rel_z - g[8:9] * rel_y
        wall_y = g[4:5] + g[8:9] * rel_x - g[6:7] * rel_z
        wall_z = g[5:6] + g[6:7] * rel_y - g[7:8] * rel_x
        correction = at(scale) * (
            at(step_x) * wall_x + at(step_y) * wall_y + at(step_z) * wall_z)
        in_row = lax.broadcasted_iota(jnp.int32, (8, 512), 0) == at(cell_x)
        values = [p.astype(F32) for p in split3(correction)] + [at(fdirs)]
        spread = jnp.concatenate(
            [jnp.where(in_row, value, 0.0) for value in values], axis=0).astype(BF16)
        dense.append(lax.dot_general(spread, targets[b], (((1,), (1,)), ((), ())),
                                     preferred_element_type=F32))
    correction = jnp.concatenate([d[0:8] + d[8:16] + d[16:24] for d in dense], axis=0)
    link_dir = jnp.concatenate([d[24:32] for d in dense], axis=0)

    region_of = {steps_of(m): k for k, m in enumerate(codes)}
    value = empty
    for q in range(1, 19):
        value = jnp.where(link_dir == float(q), star[q], value)
    links = by_block(value - correction, link_dir)
    sides = {}
    for sy, qs in ((1, plus_y), (-1, minus_y)):
        face = inbox[region_of[0, sy], 8:24, :]
        side = face
        for i, q in enumerate(qs):
            if vel[q][0]:
                side = jnp.where(lane // 8 == i, roll(face, vel[q][0], 0), side)
        sides[sy] = roll(side, 64, 1)
    margins = []
    row8, lane8 = row[0:8], lane[0:8]
    for n in range(4):
        sx = 1 if n < 2 else -1
        lines = jnp.zeros((8, 128), F32)
        for i, q in enumerate(plus_x if sx == 1 else minus_x):
            sy = vel[q][1]
            line = jnp.broadcast_to(inbox[region_of[sx, 0], 8 + i:9 + i, :], (8, 128))
            if sy:
                corner = inbox[region_of[sx, sy], 0:1, :]
                corner = roll(jnp.broadcast_to(corner, (8, 128)), 8 if sy == 1 else 0, 1)
                line = jnp.where(lane8 < 8 if sy == 1 else lane8 >= 120, corner,
                                 roll(line, 8 * sy, 1))
            lines = jnp.where(row8 == i, line, lines)
        side = sides[1 if n % 2 == 0 else -1][8 * (n // 2):8 * (n // 2) + 8]
        margin = jnp.where(wide[0:8], roll(lines, 64, 1) if n % 2 else lines, side)
        margin = jnp.where(lane8 == 112, float(n // 2), margin)
        margins.append(jnp.where(lane8 == 113, float(n % 2), margin))
    to_owners([links, margins], patch, fix_ref, patch_send, patch_recv, local_sem.at[1])
    for copy in notes:
        copy.wait_send()
    for copy in sends:
        copy.wait()


def settle(bulk_ref, fix_ref, table_in, blocks_ref, table_ref):
    table_ref[...] = table_in[...]
    lane = lax.broadcasted_iota(jnp.int32, (8, 128), 1)
    row = lax.broadcasted_iota(jnp.int32, (8, 128), 0)
    wide = lane < 64
    for a in range(bulk_ref.shape[0]):
        links, margin = fix_ref[a, 0], fix_ref[a, 1]
        turned = roll(links, 64, 1)
        link_value = jnp.where(wide, links, turned)
        link_dir = jnp.where(wide, turned, links)
        at_x = jnp.broadcast_to(margin[0:1, 112:113], (8, 128))
        at_y = jnp.broadcast_to(margin[0:1, 113:114], (8, 128))
        for p in range(10):
            value = bulk_ref[a, p]
            for half, q in ((0, p), (1, 10 + p)):
                if q > 18:
                    continue
                sx, sy, _ = vel[q]
                if sy:
                    i = (plus_y if sy == 1 else minus_y).index(q)
                    first = 64 * half + (0 if sy == 1 else 56)
                    inside = (lane >= first) & (lane < first + 8)
                    inside = inside & (at_y == (0.0 if sy == 1 else 1.0))
                    value = jnp.where(inside, roll(margin, first - 64 - 8 * i, 1), value)
                if sx:
                    i = (plus_x if sx == 1 else minus_x).index(q)
                    line = jnp.broadcast_to(margin[i:i + 1, :], (8, 128))
                    line = roll(line, 64, 1) if half else line
                    inside = (row == (0 if sx == 1 else 7)) & (wide if half == 0 else lane >= 64)
                    inside = inside & (at_x == (0.0 if sx == 1 else 1.0))
                    value = jnp.where(inside, line, value)
            wanted = jnp.where(wide, float(opp[p]) if p else -1.0,
                               float(opp[10 + p]) if p < 9 else -1.0)
            value = jnp.where(link_dir == wanted, link_value, value)
            moved = roll(value, 64, 1)
            low = jnp.where(wide, value, roll(moved, -1, 0))
            high = jnp.where(wide, moved, roll(value, -1, 0))
            for q, pairs in ((p, low), (10 + p, high)):
                if q < 19:
                    for k in range(4):
                        blocks_ref[a, q, :, k * 128:(k + 1) * 128] = pairs[2 * k:2 * k + 1, :]


def body(pdf, grains, grain_moves, owner_map, link_lists):
    nx, ny = lax.axis_size("gx"), lax.axis_size("gy")
    vmem = pl.BlockSpec(memory_space=pltpu.VMEM)
    bulk, fix, table = pl.pallas_call(
        functools.partial(kernel, nx, ny),
        out_shape=(pltpu.VMEM((nx, 10, 8, 128), F32),
                   pltpu.VMEM((nx, 2, 8, 128), F32),
                   pltpu.VMEM((26, 1, 320), F32)),
        in_specs=[pl.BlockSpec(memory_space=pltpu.HBM)] * 5,
        out_specs=(vmem, vmem, vmem),
        scratch_shapes=[
            pltpu.VMEM(pdf.shape, F32),
            pltpu.VMEM(grains.shape, F32),
            pltpu.VMEM(grain_moves.shape, jnp.int32),
            pltpu.VMEM(owner_map.shape, jnp.int32),
            pltpu.VMEM(link_lists.shape, jnp.int32),
            pltpu.SemaphoreType.DMA((5,)),
            pltpu.VMEM((19, 16, 128), F32),
            pltpu.VMEM((19, 16, 128), F32),
            pltpu.VMEM((32, 256), F32),
            pltpu.VMEM((32, 384), F32),
            pltpu.VMEM((8, 24, 128), F32),
            pltpu.VMEM((8, 24, 128), F32),
            pltpu.VMEM((nx, 10, 8, 128), F32),
            pltpu.VMEM((nx, 2, 8, 128), F32),
            pltpu.SemaphoreType.DMA((8,)),
            pltpu.SemaphoreType.DMA((8,)),
            pltpu.SemaphoreType.DMA((nx - 1,)),
            pltpu.SemaphoreType.DMA((nx - 1,)),
            pltpu.SemaphoreType.DMA((nx - 1,)),
            pltpu.SemaphoreType.DMA((nx - 1,)),
            pltpu.SemaphoreType.DMA((2,)),
        ],
        compiler_params=pltpu.CompilerParams(
            collective_id=0, has_side_effects=True, vmem_limit_bytes=60 * 1024 * 1024),
        name="slab_step",
    )(pdf, grains, grain_moves, owner_map, link_lists)
    blocks, table = pl.pallas_call(
        settle,
        out_shape=(jax.ShapeDtypeStruct((nx, 19, 1, 512), F32),
                   jax.ShapeDtypeStruct(table.shape, F32)),
        in_specs=[vmem] * 3, out_specs=(vmem, vmem),
        compiler_params=pltpu.CompilerParams(vmem_limit_bytes=24 * 1024 * 1024),
        name="settle",
    )(bulk, fix, table)
    return blocks.transpose(0, 2, 1, 3), table


def solution(mesh):
    in_specs = (
        P(None, "gx", "gy"),
        P(None, "gx", "gy"),
        P("gx", "gy"),
        P("gx", "gy"),
        P(None, "gx", "gy"),
    )
    out_specs = (P("gx", "gy", None, None), P(None, "gx", "gy"))
    return jax.shard_map(body, mesh=mesh, in_specs=in_specs, out_specs=out_specs, check_vma=False)
```

```python
import functools

import jax
import jax.numpy as jnp
import numpy as np
from jax import lax
from jax.experimental import pallas as pl
from jax.experimental.pallas import tpu as pltpu
from jax.sharding import PartitionSpec as P

MESH = pl.DeviceIdType.MESH
F32 = jnp.float32
BF16 = jnp.bfloat16

vel = [
    (0, 0, 0), (1, 0, 0), (-1, 0, 0), (0, 1, 0), (0, -1, 0), (0, 0, 1), (0, 0, -1),
    (1, 1, 0), (-1, -1, 0), (1, -1, 0), (-1, 1, 0),
    (1, 0, 1), (-1, 0, -1), (1, 0, -1), (-1, 0, 1),
    (0, 1, 1), (0, -1, -1), (0, 1, -1), (0, -1, 1),
]
opp = [0, 2, 1, 4, 3, 6, 5, 8, 7, 10, 9, 12, 11, 14, 13, 16, 15, 18, 17]
wts = [1.0 / 3.0] + [1.0 / 18.0] * 6 + [1.0 / 36.0] * 12
codes = (0, 1, 2, 3, 5, 6, 7, 8)
plus_x = [q for q in range(19) if vel[q][0] == 1]
minus_x = [q for q in range(19) if vel[q][0] == -1]
plus_y = [q for q in range(19) if vel[q][1] == 1]
minus_y = [q for q in range(19) if vel[q][1] == -1]
corner_dir = {(1, 1): 7, (-1, -1): 8, (1, -1): 9, (-1, 1): 10}


def steps_of(code):
    return code // 3 - 1, code % 3 - 1


def rows_of(code):
    dx, dy = steps_of(code)
    return 24 if dx == 0 else 16 if dy == 0 else 8


def roll(value, shift, axis):
    size = value.shape[axis]
    shift = shift % size
    return value if shift == 0 else pltpu.roll(value, shift, axis)


def split3(value):
    high = value.astype(BF16)
    rest = value - high.astype(F32)
    mid = rest.astype(BF16)
    low = (rest - mid.astype(F32)).astype(BF16)
    return high, mid, low


def collide(load):
    f = [load(q) for q in range(19)]
    sx = [f[q] for q in plus_x]
    density = functools.reduce(lambda a, b: a + b, f)

    def total(qs):
        return functools.reduce(lambda a, b: a + b, [f[q] for q in qs])

    px, mx = total(plus_x), total(minus_x)
    py, my = total(plus_y), total(minus_y)
    plus_z = [q for q in range(19) if vel[q][2] == 1]
    minus_z = [q for q in range(19) if vel[q][2] == -1]
    pz, mz = total(plus_z), total(minus_z)
    inverse = 1.0 / density
    ux, uy, uz = (px - mx) * inverse, (py - my) * inverse, (pz - mz) * inverse
    third = density * (1.0 / 3.0)
    dux, duy, duz = density * ux, density * uy, density * uz
    xx = (px + mx) - third - dux * ux
    yy = (py + my) - third - duy * uy
    zz = (pz + mz) - third - duz * uz
    xy = (f[7] + f[8]) - (f[9] + f[10]) - dux * uy
    xz = (f[11] + f[12]) - (f[13] + f[14]) - dux * uz
    yz = (f[15] + f[16]) - (f[17] + f[18]) - duy * uz
    contracted = xx * xx + yy * yy + zz * zz + 2.0 * (xy * xy + xz * xz + yz * yz)
    shear = (1.5 / 0.8) * inverse * jnp.sqrt(2.0 * contracted)
    scaled = 20.0 * shear
    viscosity = 0.01 + (0.1 - 0.01) * lax.rsqrt(jnp.sqrt(1.0 + scaled * scaled))
    omega = 1.0 / (3.0 * viscosity + 0.5)
    base = 1.0 - 1.5 * (ux * ux + uy * uy + uz * uz)
    keep = 1.0 - omega
    gain = {w: omega * density * w for w in set(wts)}
    out = []
    for q in range(19):
        c = None
        for step, u in zip(vel[q], (ux, uy, uz)):
            if step:
                term = u if step > 0 else -u
                c = term if c is None else c + term
        bracket = base if c is None else base + c * (3.0 + 4.5 * c)
        out.append(keep * f[q] + gain[wts[q]] * bracket)
    return out


def kernel(nx, ny, pdf_hbm, grains_hbm, moves_hbm, owner_hbm, links_hbm,
           bulk_ref, fix_ref, table_ref,
           pdf_ref, grains_ref, moves_ref, owner_ref, links_ref, load_sem, star, zstar, pad, tab, outbox, inbox, parcel, patch,
           note_send, note_recv, block_send, block_recv, patch_send, patch_recv, local_sem):
    gx = lax.axis_index("gx")
    gy = lax.axis_index("gy")

    def device(dx, dy):
        return (lax.rem(gx + dx + nx, nx), lax.rem(gy + dy + ny, ny))

    barrier = pltpu.get_barrier_semaphore()
    peers = [steps_of(m) for m in codes] + [(d, 0) for d in range(2, nx - 1)]
    for dx, dy in peers:
        pl.semaphore_signal(barrier, inc=1, device_id=device(dx, dy), device_id_type=MESH)

    loads = [
        pltpu.make_async_copy(source, held, load_sem.at[i])
        for i, (source, held) in enumerate((
            (grains_hbm, grains_ref), (moves_hbm, moves_ref), (pdf_hbm, pdf_ref),
            (owner_hbm, owner_ref), (links_hbm, links_ref)))
    ]
    for load in loads:
        load.start()
    lane = lax.broadcasted_iota(jnp.int32, (16, 128), 1)
    row = lax.broadcasted_iota(jnp.int32, (16, 128), 0)
    depth = lane % 8

    pad[...] = jnp.zeros_like(pad)
    for load in loads[:2]:
        load.wait()
    own = grains_ref[:, 0, :]
    pad[0:26, :] = own
    code = moves_ref[...]
    kind = lax.broadcasted_iota(jnp.int32, (16, 256), 0)
    match = jnp.where(kind == code, 1.0, 0.0)
    before = jnp.where(
        lax.broadcasted_iota(jnp.int32, (256, 256), 0)
        < lax.broadcasted_iota(jnp.int32, (256, 256), 1), 1.0, 0.0)
    counts = jnp.dot(match.astype(BF16), before.astype(BF16), preferred_element_type=F32)
    rank = jnp.sum(match * counts, axis=0, keepdims=True).astype(jnp.int32)
    region = jnp.where(code > 4, code - 1, code)
    target = jnp.where(code == 4, -1, region * 8 + rank)
    slot = lax.broadcasted_iota(jnp.int32, (64, 256), 0)
    placing = jnp.where(slot == target, 1.0, 0.0).astype(BF16)
    parts = jnp.concatenate(list(split3(pad[...])) + [jnp.zeros((32, 256), BF16)], axis=0)
    packed = lax.dot_general(placing, parts, (((1,), (1,)), ((), ())),
                             preferred_element_type=F32)
    packed = packed + roll(packed, -32, 1) + roll(packed, -64, 1)
    packed = jnp.where(lax.broadcasted_iota(jnp.int32, (64, 128), 1) < 32, packed, 0.0)

    loads[2].wait()
    collided = collide(lambda q: pdf_ref[q])
    for q in range(19):
        star[q] = collided[q]
        shifted = collided[q]
        if vel[q][2] == 1:
            shifted = jnp.where(depth == 0, roll(shifted, -7, 1), roll(shifted, 1, 1))
        elif vel[q][2] == -1:
            shifted = jnp.where(depth == 7, roll(shifted, 7, 1), roll(shifted, -1, 1))
        zstar[q] = shifted

    for k, m in enumerate(codes):
        dx, dy = steps_of(m)
        tile = packed[k * 8:(k + 1) * 8, :]
        if dx and dy:
            edge = zstar[corner_dir[dx, dy], pl.ds(15 if dx == 1 else 0, 1), :]
            if dy == -1:
                edge = roll(jnp.broadcast_to(edge, (8, 128)), 120, 1)
            tile = jnp.where(lane[0:8] >= 120, edge, tile)
        outbox[k, 0:8, :] = tile
        if dy == 0:
            for i, q in enumerate(plus_x if dx == 1 else minus_x):
                outbox[k, 8 + i:9 + i, :] = zstar[q, pl.ds(15 if dx == 1 else 0, 1), :]
        elif dx == 0:
            face = jnp.zeros((16, 128), F32)
            for i, q in enumerate(plus_y if dy == 1 else minus_y):
                moved = roll(zstar[q], 8 * i + (8 if dy == 1 else 0), 1)
                face = jnp.where(lane // 8 == i, moved, face)
            outbox[k, 8:24, :] = face

    pl.semaphore_wait(barrier, len(peers))
    notes = []
    for k, m in enumerate(codes):
        copy = pltpu.make_async_remote_copy(
            src_ref=outbox.at[k, pl.ds(0, rows_of(m))],
            dst_ref=inbox.at[k, pl.ds(0, rows_of(m))],
            send_sem=note_send.at[k], recv_sem=note_recv.at[k],
            device_id=device(*steps_of(m)), device_id_type=MESH)
        copy.start()
        notes.append(copy)

    for q in range(19):
        sx, sy, _ = vel[q]
        if sx or sy:
            zstar[q] = roll(roll(zstar[q], 8 * sy, 1), sx, 0)
    loads[3].wait()
    holds = [jnp.broadcast_to(owner_ref[n // 2:n // 2 + 1, n % 2:n % 2 + 1], (8, 128))
             for n in range(4)]
    wide = lane < 64
    sends = []

    def by_block(low, high):
        left = jnp.where(wide, low, roll(high, 64, 1))
        right = jnp.where(wide, roll(low, 64, 1), high)
        return [left[0:8], right[0:8], left[8:16], right[8:16]]

    def to_owners(tiles, box, out_ref, send_sems, recv_sems, local):
        for d in list(range(1, nx)) + [0]:
            to = lax.rem(gx + d, nx)
            mine = [hold == to for hold in holds]
            for p, tile in enumerate(tiles):
                value = jnp.zeros((8, 128), F32)
                for n in range(4):
                    value = jnp.where(mine[n], tile[n], value)
                box[d, p] = value
            if d:
                copy = pltpu.make_async_remote_copy(
                    src_ref=box.at[d], dst_ref=out_ref.at[gx],
                    send_sem=send_sems.at[d - 1], recv_sem=recv_sems.at[d - 1],
                    device_id=(to, gy), device_id_type=MESH)
            else:
                copy = pltpu.make_async_copy(box.at[0], out_ref.at[gx], local)
            copy.start()
            sends.append(copy)

    empty = jnp.zeros((16, 128), F32)
    to_owners([by_block(zstar[p], zstar[10 + p] if p < 9 else empty) for p in range(10)],
              parcel, bulk_ref, block_send, block_recv, local_sem.at[0])

    kept = own * jnp.where(code == 4, 1.0, 0.0)
    tab[...] = jnp.zeros_like(tab)
    tab[0:26, 0:256] = kept
    loads[4].wait()
    cells, dirs, slots = links_ref[0], links_ref[1], links_ref[2]

    def step_along(axis):
        value = jnp.zeros((2, 512), F32)
        for q in range(1, 19):
            if vel[q][axis]:
                value = jnp.where(dirs == q, float(vel[q][axis]), value)
        return value

    step_x, step_y, step_z = step_along(0), step_along(1), step_along(2)
    half = lax.broadcasted_iota(jnp.int32, (2, 512), 1) // 256
    bx = lax.broadcasted_iota(jnp.int32, (2, 512), 0)
    cell_x, cell_y, cell_z = cells // 64, cells // 8 % 8, cells % 8
    mid_x = ((gx * 2 + bx) * 8 + cell_x).astype(F32) + 0.5 * step_x
    mid_y = ((gy * 2 + half) * 8 + cell_y).astype(F32) + 0.5 * step_y
    mid_z = cell_z.astype(F32) + 0.5 * step_z
    scale = jnp.where(dirs < 7, 6.0 / 18.0, 6.0 / 36.0)
    place = half * 64 + cells % 64
    fdirs = dirs.astype(F32)

    features = jnp.concatenate(list(split3(tab[0:16, 0:256])), axis=0)
    resting, arriving, targets = [], [], []
    for b in range(2):
        slot = slots[b:b + 1, :]
        chosen = jnp.where(
            lax.broadcasted_iota(jnp.int32, (256, 512), 0) == slot, 1.0, 0.0).astype(BF16)
        resting.append(jnp.dot(features, chosen, preferred_element_type=F32))
        arriving.append(jnp.where(
            lax.broadcasted_iota(jnp.int32, (128, 512), 0) + 256 == slot,
            1.0, 0.0).astype(BF16))
        targets.append(jnp.where(
            lax.broadcasted_iota(jnp.int32, (128, 512), 0) == place[b:b + 1, :],
            1.0, 0.0).astype(BF16))

    for copy in notes:
        copy.wait_recv()

    incoming = inbox[:, 0:8, :].reshape(64, 128)
    incoming = jnp.concatenate([incoming, jnp.zeros((64, 128), F32)], axis=0).T
    tab[0:26, 256:384] = incoming[0:26, :]
    table_ref[:, 0, :] = tab[0:26, 0:320]
    features = jnp.concatenate(list(split3(tab[0:16, 256:384])), axis=0)
    dense = []
    for b in range(2):
        def at(value):
            return value[b:b + 1, :]

        g = resting[b] + jnp.dot(features, arriving[b], preferred_element_type=F32)
        g = g[0:16] + g[16:32] + g[32:48]
        rel_x, rel_y, rel_z = at(mid_x) - g[0:1], at(mid_y) - g[1:2], at(mid_z) - g[2:3]
        wall_x = g[3:4] + g[7:8] * rel_z - g[8:9] * rel_y
        wall_y = g[4:5] + g[8:9] * rel_x - g[6:7] * rel_z
        wall_z = g[5:6] + g[6:7] * rel_y - g[7:8] * rel_x
        correction = at(scale) * (
            at(step_x) * wall_x + at(step_y) * wall_y + at(step_z) * wall_z)
        in_row = lax.broadcasted_iota(jnp.int32, (8, 512), 0) == at(cell_x)
        values = [p.astype(F32) for p in split3(correction)] + [at(fdirs)]
        spread = jnp.concatenate(
            [jnp.where(in_row, value, 0.0) for value in values], axis=0).astype(BF16)
        dense.append(lax.dot_general(spread, targets[b], (((1,), (1,)), ((), ())),
                                     preferred_element_type=F32))
    correction = jnp.concatenate([d[0:8] + d[8:16] + d[16:24] for d in dense], axis=0)
    link_dir = jnp.concatenate([d[24:32] for d in dense], axis=0)

    region_of = {steps_of(m): k for k, m in enumerate(codes)}
    value = empty
    for q in range(1, 19):
        value = jnp.where(link_dir == float(q), star[q], value)
    links = by_block(value - correction, link_dir)
    sides = {}
    for sy, qs in ((1, plus_y), (-1, minus_y)):
        face = inbox[region_of[0, sy], 8:24, :]
        side = face
        for i, q in enumerate(qs):
            if vel[q][0]:
                side = jnp.where(lane // 8 == i, roll(face, vel[q][0], 0), side)
        sides[sy] = roll(side, 64, 1)
    margins = []
    row8, lane8 = row[0:8], lane[0:8]
    for n in range(4):
        sx = 1 if n < 2 else -1
        lines = jnp.zeros((8, 128), F32)
        for i, q in enumerate(plus_x if sx == 1 else minus_x):
            sy = vel[q][1]
            line = jnp.broadcast_to(inbox[region_of[sx, 0], 8 + i:9 + i, :], (8, 128))
            if sy:
                corner = inbox[region_of[sx, sy], 0:1, :]
                corner = roll(jnp.broadcast_to(corner, (8, 128)), 8 if sy == 1 else 0, 1)
                line = jnp.where(lane8 < 8 if sy == 1 else lane8 >= 120, corner,
                                 roll(line, 8 * sy, 1))
            lines = jnp.where(row8 == i, line, lines)
        side = sides[1 if n % 2 == 0 else -1][8 * (n // 2):8 * (n // 2) + 8]
        margin = jnp.where(wide[0:8], roll(lines, 64, 1) if n % 2 else lines, side)
        margin = jnp.where(lane8 == 112, float(n // 2), margin)
        margins.append(jnp.where(lane8 == 113, float(n % 2), margin))
    to_owners([links, margins], patch, fix_ref, patch_send, patch_recv, local_sem.at[1])
    for copy in notes:
        copy.wait_send()
    for copy in sends:
        copy.wait()


def settle(bulk_ref, fix_ref, table_in, blocks_out, table_out, blocks_ref, sem):
    count = bulk_ref.shape[0]
    stores = [pltpu.make_async_copy(table_in, table_out, sem.at[count])]
    stores[0].start()
    lane = lax.broadcasted_iota(jnp.int32, (8, 128), 1)
    row = lax.broadcasted_iota(jnp.int32, (8, 128), 0)
    wide = lane < 64
    for a in range(bulk_ref.shape[0]):
        links, margin = fix_ref[a, 0], fix_ref[a, 1]
        turned = roll(links, 64, 1)
        link_value = jnp.where(wide, links, turned)
        link_dir = jnp.where(wide, turned, links)
        at_x = jnp.broadcast_to(margin[0:1, 112:113], (8, 128))
        at_y = jnp.broadcast_to(margin[0:1, 113:114], (8, 128))
        for p in range(10):
            value = bulk_ref[a, p]
            for half, q in ((0, p), (1, 10 + p)):
                if q > 18:
                    continue
                sx, sy, _ = vel[q]
                if sy:
                    i = (plus_y if sy == 1 else minus_y).index(q)
                    first = 64 * half + (0 if sy == 1 else 56)
                    inside = (lane >= first) & (lane < first + 8)
                    inside = inside & (at_y == (0.0 if sy == 1 else 1.0))
                    value = jnp.where(inside, roll(margin, first - 64 - 8 * i, 1), value)
                if sx:
                    i = (plus_x if sx == 1 else minus_x).index(q)
                    line = jnp.broadcast_to(margin[i:i + 1, :], (8, 128))
                    line = roll(line, 64, 1) if half else line
                    inside = (row == (0 if sx == 1 else 7)) & (wide if half == 0 else lane >= 64)
                    inside = inside & (at_x == (0.0 if sx == 1 else 1.0))
                    value = jnp.where(inside, line, value)
            wanted = jnp.where(wide, float(opp[p]) if p else -1.0,
                               float(opp[10 + p]) if p < 9 else -1.0)
            value = jnp.where(link_dir == wanted, link_value, value)
            moved = roll(value, 64, 1)
            low = jnp.where(wide, value, roll(moved, -1, 0))
            high = jnp.where(wide, moved, roll(value, -1, 0))
            for q, pairs in ((p, low), (10 + p, high)):
                if q < 19:
                    for k in range(4):
                        blocks_ref[a, q, :, k * 128:(k + 1) * 128] = pairs[2 * k:2 * k + 1, :]
        store = pltpu.make_async_copy(blocks_ref.at[a], blocks_out.at[a], sem.at[a])
        store.start()
        stores.append(store)
    for store in stores:
        store.wait()


def body(pdf, grains, grain_moves, owner_map, link_lists):
    nx, ny = lax.axis_size("gx"), lax.axis_size("gy")
    vmem = pl.BlockSpec(memory_space=pltpu.VMEM)
    bulk, fix, table = pl.pallas_call(
        functools.partial(kernel, nx, ny),
        out_shape=(pltpu.VMEM((nx, 10, 8, 128), F32),
                   pltpu.VMEM((nx, 2, 8, 128), F32),
                   pltpu.VMEM((26, 1, 320), F32)),
        in_specs=[pl.BlockSpec(memory_space=pltpu.HBM)] * 5,
        out_specs=(vmem, vmem, vmem),
        scratch_shapes=[
            pltpu.VMEM(pdf.shape, F32),
            pltpu.VMEM(grains.shape, F32),
            pltpu.VMEM(grain_moves.shape, jnp.int32),
            pltpu.VMEM(owner_map.shape, jnp.int32),
            pltpu.VMEM(link_lists.shape, jnp.int32),
            pltpu.SemaphoreType.DMA((5,)),
            pltpu.VMEM((19, 16, 128), F32),
            pltpu.VMEM((19, 16, 128), F32),
            pltpu.VMEM((32, 256), F32),
            pltpu.VMEM((32, 384), F32),
            pltpu.VMEM((8, 24, 128), F32),
            pltpu.VMEM((8, 24, 128), F32),
            pltpu.VMEM((nx, 10, 8, 128), F32),
            pltpu.VMEM((nx, 2, 8, 128), F32),
            pltpu.SemaphoreType.DMA((8,)),
            pltpu.SemaphoreType.DMA((8,)),
            pltpu.SemaphoreType.DMA((nx - 1,)),
            pltpu.SemaphoreType.DMA((nx - 1,)),
            pltpu.SemaphoreType.DMA((nx - 1,)),
            pltpu.SemaphoreType.DMA((nx - 1,)),
            pltpu.SemaphoreType.DMA((2,)),
        ],
        compiler_params=pltpu.CompilerParams(
            collective_id=0, has_side_effects=True, vmem_limit_bytes=60 * 1024 * 1024),
        name="slab_step",
    )(pdf, grains, grain_moves, owner_map, link_lists)
    blocks, table = pl.pallas_call(
        settle,
        out_shape=(jax.ShapeDtypeStruct((nx, 19, 1, 512), F32),
                   jax.ShapeDtypeStruct(table.shape, F32)),
        in_specs=[vmem] * 3, out_specs=(pl.BlockSpec(memory_space=pltpu.HBM),) * 2,
        scratch_shapes=[pltpu.VMEM((nx, 19, 1, 512), F32),
                        pltpu.SemaphoreType.DMA((nx + 1,))],
        compiler_params=pltpu.CompilerParams(vmem_limit_bytes=24 * 1024 * 1024),
        name="settle",
    )(bulk, fix, table)
    return blocks.transpose(0, 2, 1, 3), table


def solution(mesh):
    in_specs = (
        P(None, "gx", "gy"),
        P(None, "gx", "gy"),
        P("gx", "gy"),
        P("gx", "gy"),
        P(None, "gx", "gy"),
    )
    out_specs = (P("gx", "gy", None, None), P(None, "gx", "gy"))
    return jax.shard_map(body, mesh=mesh, in_specs=in_specs, out_specs=out_specs, check_vma=False)
```
